128 devices in a mesh: point: 16 (over x, z), cent: 8 (over y, core).
Axes of the slice: x: 4, y: 4, z: 4, core: 2. Of those that a mesh axis runs over, the one named last changes fastest.
Arguments:
- points: bfloat16 [65536, 1024], P(('point', 'cent')), may hold values from -0.1875 to 0.1875
- assign: int32 [65536], P(('point', 'cent')), may hold values from 0 to 8191
- old_centroids: bfloat16 [8192, 1024], P('cent'), may hold values from -0.1875 to 0.1875
Outputs:
- new_centroids: bfloat16 [8192, 1024], P('cent')
- distances: float32 [65536, 8192], P('point', 'cent')
The draws below stay inside these ranges and needn't reach their ends.
All inputs are finite; a program needn't handle non-finite values.
Results may differ from the reference program's by a relative error of at most 0.008.
Values may be sent and summed in bfloat16 or wider, within the bound.
A program may use at most 128 MiB of HBM per device.

```python
import jax
import jax.numpy as jnp
from jax import lax

D = 1024
K = 8192
NPTS = 65536


def draw_assign(key, part):
    key = jax.random.fold_in(key, 7)
    order_key, chance_key, heavy_key, flip_key = jax.random.split(key, 4)
    ordering = jax.random.permutation(order_key, K).astype(jnp.int32)
    position = jnp.arange(NPTS, dtype=jnp.int32) % K
    chance = jax.random.randint(chance_key, (NPTS,), 0, 16)
    heavy_slot = jax.random.randint(heavy_key, (NPTS,), 0, K // 128)
    flipper = jax.random.randint(flip_key, (), 1, 15)
    regular = ordering[position]
    empty_id = (regular ^ flipper) % 16 == 0
    chosen = jnp.where((chance == 0) | empty_id, ordering[heavy_slot], regular)
    return chosen.astype(jnp.int32)


def steps_of(key, extent, pieces, least, top_value):
    loudness, own = 1.0, jax.random.fold_in(key, 6)
    for dim, blocks in pieces:
        heights = jnp.exp(jax.random.uniform(jax.random.fold_in(own, dim), (blocks,), jnp.float32, least / len(pieces), top_value / len(pieces)))
        loudness = loudness * jnp.repeat(heights, extent[dim] // blocks).reshape([-1 if axis == dim else 1 for axis in range(len(extent))])
    return loudness


def gaussian(key, dims, width, reach, pieces=(), kind=jnp.bfloat16):
    factor_of = steps_of(key, dims, pieces, -0.22, 0.18) if pieces else 1.0
    entries = jax.random.normal(key, dims, jnp.float32) * width * factor_of
    return jnp.minimum(jnp.maximum(entries, -reach), reach).astype(kind)


def setup_inputs(seed: int = 0) -> dict:
    key_of = jax.random.split(jax.random.key(seed), 4)
    points = gaussian(key_of[0], (NPTS, D), D ** -0.5, 0.1875, ((0, 128),))
    assign = draw_assign(jax.random.fold_in(key_of[3], 71), 0)
    old_centroids = gaussian(key_of[2], (K, D), D ** -0.5, 0.1875, ((0, 8),))
    return {"points": points, "assign": assign, "old_centroids": old_centroids}


def reference(points, assign, old_centroids):
    widened = points.astype(jnp.float32)
    totals = jax.ops.segment_sum(widened, assign, num_segments=K)
    counts = jax.ops.segment_sum(jnp.ones(assign.shape, jnp.float32), assign, num_segments=K)
    old_wide = old_centroids.astype(jnp.float32)
    mean_rows = totals / jnp.maximum(counts, 1.0)[:, None]
    blended = jnp.where((counts > 0.0)[:, None], 0.5 * mean_rows + 0.5 * old_wide, old_wide)
    scaling = lax.rsqrt(lax.optimization_barrier(jnp.sum(blended * blended, axis=1)) + 1e-06)
    new_centroids = (blended * scaling[:, None]).astype(jnp.bfloat16)
    cent_sq = lax.optimization_barrier(jnp.sum(jnp.square(new_centroids.astype(jnp.float32)), axis=1))
    block_rows = min(points.shape[0], 256)
    blocks = points.reshape(points.shape[0] // block_rows, block_rows, points.shape[1])

    def one_block(block_pts):
        products = jnp.dot(block_pts, new_centroids.T, preferred_element_type=jnp.float32)
        point_sq = lax.optimization_barrier(jnp.sum(jnp.square(block_pts.astype(jnp.float32)), axis=1))
        return point_sq[:, None] + cent_sq[None, :] - 2.0 * products
    distances = lax.map(one_block, blocks).reshape(points.shape[0], K)
    return (new_centroids, distances)
```

```python
import functools

import jax
import jax.numpy as jnp
from jax import lax
from jax.experimental import pallas as pl
from jax.experimental.pallas import tpu as pltpu
from jax.sharding import PartitionSpec as P

MESH = pl.DeviceIdType.MESH
F32, BF16 = jnp.float32, jnp.bfloat16
LANES = 128
GROUPS = (2, 2, 2, 1, 1)
DIGITS = 128


class Wires:
    def __init__(self, send, recv, local):
        self.send, self.recv, self.local = send, recv, local
        self.n_remote = self.n_local = 0
        self.sent, self.stored = [], []

    def remote(self, src, dst, target):
        index = self.n_remote
        self.n_remote += 1
        copy = pltpu.make_async_remote_copy(
            src_ref=src, dst_ref=dst, send_sem=self.send.at[index], recv_sem=self.recv.at[index],
            device_id=target, device_id_type=MESH,
        )
        copy.start()
        self.sent.append(copy)
        return copy

    def here(self, src, dst):
        copy = pltpu.make_async_copy(src, dst, self.local.at[self.n_local])
        self.n_local += 1
        copy.start()
        return copy


def gather_chunk(wires, buf, slot, up, down, sibling):
    rows = buf(0).shape[0]
    half = rows // 2

    def piece(k, part):
        return buf(k).at[pl.ds(part * half, half)]

    from_below = wires.remote(buf(0), buf(1), up)
    from_above = wires.remote(buf(0), buf(2), down)
    shared = [wires.remote(buf(0), buf(4), sibling)]
    yield
    from_below.wait_recv()
    far_a = wires.remote(piece(1, 0), piece(3, 0), up)
    shared.append(wires.remote(buf(1), buf(5), sibling))
    from_above.wait_recv()
    far_b = wires.remote(piece(2, 1), piece(3, 1), down)
    shared.append(wires.remote(buf(2), buf(6), sibling))
    yield
    far_a.wait_recv()
    shared.append(wires.remote(piece(3, 0), piece(7, 0), sibling))
    far_b.wait_recv()
    shared.append(wires.remote(piece(3, 1), piece(7, 1), sibling))
    yield
    for copy in shared:
        copy.wait_recv()
    yield


def gather_labels(wires, lab, up, down, sibling):
    from_below = wires.remote(lab.at[0], lab.at[1], up)
    from_above = wires.remote(lab.at[0], lab.at[2], down)
    shared = [wires.remote(lab.at[0], lab.at[4], sibling)]
    yield
    from_below.wait_recv()
    far = wires.remote(lab.at[1], lab.at[3], up)
    shared.append(wires.remote(lab.at[1], lab.at[5], sibling))
    from_above.wait_recv()
    shared.append(wires.remote(lab.at[2], lab.at[6], sibling))
    yield
    far.wait_recv()
    shared.append(wires.remote(lab.at[3], lab.at[7], sibling))
    yield
    for copy in shared:
        copy.wait_recv()
    yield


def add(*terms):
    total = terms[0].astype(F32)
    for term in terms[1:]:
        total = total + term.astype(F32)
    return total


def reduce_half(wires, base, first, second, first_ids, second_ids, part, land, cent, finish):
    a_up, a_down = first_ids
    b_up, b_down = second_ids

    def outer(k, start=0, size=128):
        return pl.ds(pl.multiple_of(base + lax.rem(first + 4 + k, 4) * 128 + start, 16), size)

    def inner(k, start=0, size=32):
        return pl.ds(pl.multiple_of(base + first * 128 + lax.rem(second + 4 + k, 4) * 32 + start, 16), size)

    def landing(start, size):
        return land.at[pl.ds(start, size)]

    one_a = wires.remote(part.at[outer(2, 0, 64)], landing(0, 64), a_up)
    one_b = wires.remote(part.at[outer(2, 64, 64)], landing(64, 64), a_down)
    yield
    one_a.wait_recv()
    part[outer(1, 0, 64)] = add(part[outer(1, 0, 64)], land[0:64]).astype(BF16)
    two_a = wires.remote(part.at[outer(1)], landing(128, 128), a_up)
    one_b.wait_recv()
    part[outer(-1, 64, 64)] = add(part[outer(-1, 64, 64)], land[64:128]).astype(BF16)
    two_b = wires.remote(part.at[outer(-1)], landing(256, 128), a_down)
    yield
    two_a.wait_recv()
    two_b.wait_recv()
    part[outer(0)] = add(part[outer(0)], land[128:256], land[256:384]).astype(BF16)
    three_a = wires.remote(part.at[inner(2, 0, 16)], landing(384, 16), b_up)
    three_b = wires.remote(part.at[inner(2, 16, 16)], landing(400, 16), b_down)
    yield
    three_a.wait_recv()
    part[inner(1, 0, 16)] = add(part[inner(1, 0, 16)], land[384:400]).astype(BF16)
    four_a = wires.remote(part.at[inner(1)], landing(416, 32), b_up)
    three_b.wait_recv()
    part[inner(-1, 16, 16)] = add(part[inner(-1, 16, 16)], land[400:416]).astype(BF16)
    four_b = wires.remote(part.at[inner(-1)], landing(448, 32), b_down)
    yield
    four_a.wait_recv()
    four_b.wait_recv()
    cent[inner(0)] = finish(add(part[inner(0)], land[416:448], land[448:480]))
    five_a = wires.remote(cent.at[inner(0)], cent.at[inner(0)], b_up)
    five_b = wires.remote(cent.at[inner(0)], cent.at[inner(0)], b_down)
    yield
    five_a.wait_recv()
    six_a = wires.remote(cent.at[inner(-1, 0, 16)], cent.at[inner(-1, 0, 16)], b_up)
    five_b.wait_recv()
    six_b = wires.remote(cent.at[inner(1, 16, 16)], cent.at[inner(1, 16, 16)], b_down)
    yield
    six_a.wait_recv()
    six_b.wait_recv()
    seven_a = wires.remote(cent.at[outer(0)], cent.at[outer(0)], a_up)
    seven_b = wires.remote(cent.at[outer(0)], cent.at[outer(0)], a_down)
    yield
    seven_a.wait_recv()
    eight_a = wires.remote(cent.at[outer(-1, 0, 64)], cent.at[outer(-1, 0, 64)], a_up)
    seven_b.wait_recv()
    eight_b = wires.remote(cent.at[outer(1, 64, 64)], cent.at[outer(1, 64, 64)], a_down)
    yield
    eight_a.wait_recv()
    eight_b.wait_recv()
    yield


def centroid_kernel(points, labels, old, all_points, blended, pts, lab, onehot, old_rows, weights, *rest):
    n_groups = len(GROUPS)
    parts, lands, cents = rest[:n_groups], rest[n_groups : 2 * n_groups], rest[2 * n_groups : 3 * n_groups]
    send, recv, local = rest[3 * n_groups :]
    wires = Wires(send, recv, local)
    p, c = lax.axis_index("point"), lax.axis_index("cent")
    x, z, y, core = p // 4, lax.rem(p, 4), c // 2, lax.rem(c, 2)

    def ring(k, by):
        return lax.rem(k + 4 + by, 4)

    up, down = ({"cent": ring(y, by) * 2 + core} for by in (1, -1))
    sibling = {"cent": y * 2 + 1 - core}
    x_ids = tuple({"point": ring(x, by) * 4 + z} for by in (1, -1))
    z_ids = tuple({"point": x * 4 + ring(z, by)} for by in (1, -1))

    rows = points.shape[0]
    loads = [wires.here(labels, lab.at[0]), wires.here(points, pts.at[pl.ds(0, rows)])]
    row_a = pl.multiple_of(x * 128 + z * 32, 32)
    row_b = pl.multiple_of(512 + z * 128 + x * 32, 32)
    old_loads = [wires.here(old.at[pl.ds(row_a, 32)], old_rows.at[0]), wires.here(old.at[pl.ds(row_b, 32)], old_rows.at[1])]

    barrier = pltpu.get_barrier_semaphore()
    for other in (up, down, sibling, *x_ids, *z_ids):
        pl.semaphore_signal(barrier, inc=1, device_id=other, device_id_type=MESH)
    pl.semaphore_wait(barrier, 7)
    for load in loads:
        load.wait()

    n_chunks = pts.shape[1] // LANES
    gathers = []

    def start_gather(t):
        if t < n_chunks:
            buf = lambda k: pts.at[pl.ds(k * rows, rows), pl.ds(t * LANES, LANES)]
            gathers.append(gather_chunk(wires, buf, None, up, down, sibling))
            next(gathers[t])

    label_gather = gather_labels(wires, lab, up, down, sibling)
    next(label_gather)
    start_gather(0)
    start_gather(1)
    for _ in range(3):
        next(label_gather)

    n_rows = onehot.shape[0]
    first_id = c * n_rows
    tile = 64

    @pl.loop(0, n_rows // tile)
    def _(r):
        row = pl.multiple_of(r * tile, tile)
        ids = first_id + row + lax.broadcasted_iota(jnp.int32, (tile, rows), 0)
        for k in range(8):
            same = ids == lab[k, 0:1, :]
            onehot[pl.ds(row, tile), k * rows : (k + 1) * rows] = jnp.where(same, 1.0, 0.0).astype(BF16)

    width0 = GROUPS[0] * LANES
    ones = jnp.ones((onehot.shape[1], DIGITS), BF16)

    @pl.loop(0, n_rows // 256)
    def _(r):
        row = pl.ds(pl.multiple_of(r * 256, 256), 256)
        count = jnp.dot(onehot[row, :], ones, preferred_element_type=F32).astype(jnp.int32)
        place = lax.broadcasted_iota(jnp.int32, count.shape, 1) & 3
        digit = lax.shift_right_logical(count, place * 4) & 15
        parts[0][row, width0:] = digit.astype(F32).astype(BF16)

    for load in old_loads:
        load.wait()

    def finisher(g, half):
        start = sum(GROUPS[:g]) * LANES
        width = GROUPS[g] * LANES

        def finish(total):
            if g == 0:
                place = lax.broadcasted_iota(jnp.int32, (32, DIGITS), 1)
                scale = jnp.where(place == 0, 1.0, jnp.where(place == 1, 16.0, jnp.where(place == 2, 256.0, 4096.0)))
                digits = jnp.where(place < 4, total[:, width:] * scale, 0.0)
                count = jnp.sum(digits, axis=1, keepdims=True)
                weights[half, 0] = jnp.broadcast_to(jnp.where(count > 0.0, 0.5 / jnp.maximum(count, 1.0), 0.0), (32, 128))
                weights[half, 1] = jnp.broadcast_to(jnp.where(count > 0.0, 0.5, 1.0), (32, 128))
            new_w, old_w = weights[half, 0][:, 0:1], weights[half, 1][:, 0:1]
            old_part = old_rows[half, :, start : start + width].astype(F32)
            return (total[:, :width] * new_w + old_part * old_w).astype(BF16)

        return finish

    flying = []

    def start_group(g):
        start, width = sum(GROUPS[:g]) * LANES, GROUPS[g] * LANES
        part = parts[g]

        @pl.loop(0, n_rows // 256)
        def _(r):
            row = pl.ds(pl.multiple_of(r * 256, 256), 256)
            sums = jnp.dot(onehot[row, :], pts[:, start : start + width], preferred_element_type=F32)
            part[row, 0:width] = sums.astype(BF16)

        halves = (
            reduce_half(wires, 0, x, z, x_ids, z_ids, part, lands[g].at[0], cents[g], finisher(g, 0)),
            reduce_half(wires, 512, z, x, z_ids, x_ids, part, lands[g].at[1], cents[g], finisher(g, 1)),
        )
        for half in halves:
            next(half)
        flying.append((g, halves))

    stores = []

    def advance():
        for entry in list(flying):
            g, halves = entry
            for half in halves:
                next(half)
            entry_steps[g] = entry_steps.get(g, 0) + 1
            if entry_steps[g] == 8:
                flying.remove(entry)
                start, width = sum(GROUPS[:g]) * LANES, GROUPS[g] * LANES
                stores.append(wires.here(cents[g], blended.at[:, pl.ds(start, width)]))

    entry_steps = {}
    ends = [sum(GROUPS[: g + 1]) for g in range(n_groups)]
    for t in range(n_chunks + 1):
        if t < n_chunks:
            next(gathers[t])
            start_gather(t + 2)
        advance()
        if t >= 1:
            next(gathers[t - 1])
            advance()
            next(gathers[t - 1])
            stores.append(wires.here(pts.at[:, pl.ds((t - 1) * LANES, LANES)], all_points.at[:, pl.ds((t - 1) * LANES, LANES)]))
            if t in ends:
                start_group(ends.index(t))
    while flying:
        advance()
    for copy in wires.sent:
        copy.wait_send()
    for copy in stores:
        copy.wait()


def distance_kernel(points, blended, new, out, cent_sq):
    @pl.when(pl.program_id(0) == 0)
    def _():
        ones = jnp.ones((8, blended.shape[1]), BF16)
        tile = 128

        for r in range(blended.shape[0] // tile):
            row = pl.ds(r * tile, tile)
            wide = blended[row, :].astype(F32)
            scale = lax.rsqrt(jnp.sum(wide * wide, axis=1, keepdims=True) + 1e-06)
            rounded = (wide * scale).astype(BF16)
            new[row, :] = rounded
            square = jnp.square(rounded.astype(F32))
            high = square.astype(BF16)
            low = (square - high.astype(F32)).astype(BF16)
            nt = (((1,), (1,)), ((), ()))
            cent_sq[:, r * tile : (r + 1) * tile] = lax.dot_general(
                ones, high, nt, preferred_element_type=F32
            ) + lax.dot_general(ones, low, nt, preferred_element_type=F32)

    block = points[...]
    wide = block.astype(F32)
    point_sq = jnp.sum(wide * wide, axis=1, keepdims=True)
    products = lax.dot_general(block, new[...], (((1,), (1,)), ((), ())), preferred_element_type=F32)
    out[...] = (point_sq + cent_sq[0:1, :]) - 2.0 * products


def block_of(k):
    c = lax.axis_index("cent")
    y, core = c // 2, lax.rem(c, 2)
    far, other = lax.rem(k, 4), k // 4
    shift = jnp.where(far == 0, 0, jnp.where(far == 1, 3, jnp.where(far == 2, 1, 2)))
    side = jnp.where(other == 0, core, 1 - core)
    return lax.rem(y + shift, 4) * 2 + side


def shards(points, assign, old_centroids):
    rows, width = points.shape
    n_rows = old_centroids.shape[0]
    labels = jnp.broadcast_to(assign[None, :], (8, rows))
    group = 8 * rows
    widths = [n * LANES for n in GROUPS]
    sums = [w + (DIGITS if g == 0 else 0) for g, w in enumerate(widths)]
    n_remote = 9 * (width // LANES) + 8 + 32 * len(GROUPS)
    everywhere = pl.BlockSpec(memory_space=pl.ANY)
    all_points, blended = pl.pallas_call(
        centroid_kernel,
        out_shape=(jax.ShapeDtypeStruct((group, width), BF16), jax.ShapeDtypeStruct((n_rows, width), BF16)),
        in_specs=[everywhere] * 3,
        out_specs=(everywhere, everywhere),
        scratch_shapes=[
            pltpu.VMEM((group, width), BF16),
            pltpu.VMEM((8, 8, rows), jnp.int32),
            pltpu.VMEM((n_rows, group), BF16),
            pltpu.VMEM((2, 32, width), BF16),
            pltpu.VMEM((2, 2, 32, 128), F32),
            *[pltpu.VMEM((n_rows, w), BF16) for w in sums],
            *[pltpu.VMEM((2, 480, w), BF16) for w in sums],
            *[pltpu.VMEM((n_rows, w), BF16) for w in widths],
            pltpu.SemaphoreType.DMA((n_remote,)),
            pltpu.SemaphoreType.DMA((n_remote,)),
            pltpu.SemaphoreType.DMA((4 + width // LANES + len(GROUPS),)),
        ],
        compiler_params=pltpu.CompilerParams(
            collective_id=0, has_side_effects=True, vmem_limit_bytes=40 * 2**20
        ),
        cost_estimate=pl.CostEstimate(flops=2 * n_rows * group * width, bytes_accessed=2 * group * width, transcendentals=0),
    )(points, labels, old_centroids)
    new_centroids, distances = pl.pallas_call(
        distance_kernel,
        grid=(8,),
        out_shape=(jax.ShapeDtypeStruct((n_rows, width), BF16), jax.ShapeDtypeStruct((group, n_rows), F32)),
        in_specs=[
            pl.BlockSpec((rows, width), lambda k: (k, 0)),
            pl.BlockSpec((n_rows, width), lambda k: (0, 0)),
        ],
        out_specs=(
            pl.BlockSpec((n_rows, width), lambda k: (0, 0)),
            pl.BlockSpec((rows, n_rows), lambda k: (block_of(k), 0)),
        ),
        scratch_shapes=[pltpu.VMEM((8, n_rows), F32)],
        compiler_params=pltpu.CompilerParams(vmem_limit_bytes=40 * 2**20),
        cost_estimate=pl.CostEstimate(
            flops=2 * n_rows * group * width, bytes_accessed=4 * group * n_rows + 2 * group * width, transcendentals=0
        ),
    )(all_points, blended)
    return new_centroids, distances


def solution(mesh):
    return jax.shard_map(
        shards,
        mesh=mesh,
        in_specs=(P(("point", "cent"), None), P(("point", "cent")), P("cent", None)),
        out_specs=(P("cent", None), P("point", "cent")),
        check_vma=False,
    )
```

```python
import functools

import jax
import jax.numpy as jnp
from jax import lax
from jax.experimental import pallas as pl
from jax.experimental.pallas import tpu as pltpu
from jax.sharding import PartitionSpec as P

MESH = pl.DeviceIdType.MESH
F32, BF16 = jnp.float32, jnp.bfloat16
LANES = 128
GROUPS = (2, 2, 2, 1, 1)
DIGITS = 128


class Wires:
    def __init__(self, send, recv, local):
        self.send, self.recv, self.local = send, recv, local
        self.n_remote = self.n_local = 0
        self.sent, self.stored = [], []

    def remote(self, src, dst, target):
        index = self.n_remote
        self.n_remote += 1
        copy = pltpu.make_async_remote_copy(
            src_ref=src, dst_ref=dst, send_sem=self.send.at[index], recv_sem=self.recv.at[index],
            device_id=target, device_id_type=MESH,
        )
        copy.start()
        self.sent.append(copy)
        return copy

    def here(self, src, dst):
        copy = pltpu.make_async_copy(src, dst, self.local.at[self.n_local])
        self.n_local += 1
        copy.start()
        return copy


def gather_chunk(wires, buf, up, down, sibling):
    half = buf(0).shape[0] // 2

    def piece(k, part):
        return buf(k).at[pl.ds(part * half, half)]

    from_below = wires.remote(buf(0), buf(1), up)
    from_above = wires.remote(buf(0), buf(2), down)
    near = [wires.remote(buf(0), buf(3), sibling)]
    yield
    from_below.wait_recv()
    far_a = wires.remote(piece(1, 0), piece(6, 0), up)
    from_above.wait_recv()
    far_b = wires.remote(piece(2, 1), piece(6, 1), down)
    near.append(wires.remote(buf(1), buf(4), sibling))
    near.append(wires.remote(buf(2), buf(5), sibling))
    yield
    for copy in near:
        copy.wait_recv()
    yield
    far_a.wait_recv()
    far = [wires.remote(piece(6, 0), piece(7, 0), sibling)]
    far_b.wait_recv()
    far.append(wires.remote(piece(6, 1), piece(7, 1), sibling))
    yield
    for copy in far:
        copy.wait_recv()
    yield


def gather_labels(wires, lab, up, down, across, sibling):
    first = [wires.remote(lab.at[0], lab.at[k], target) for k, target in ((6, across), (1, up), (2, down))]
    near = [wires.remote(lab.at[0], lab.at[3], sibling)]
    yield
    for copy, k, to in zip(first[1:] + first[:1], (1, 2, 6), (4, 5, 7)):
        copy.wait_recv()
        near.append(wires.remote(lab.at[k], lab.at[to], sibling))
    yield
    for copy in near:
        copy.wait_recv()
    yield


def add(*terms):
    total = terms[0].astype(F32)
    for term in terms[1:]:
        total = total + term.astype(F32)
    return total


def reduce_half(wires, base, first, second, first_ids, second_ids, part, land, cent, finish):
    order = (2, 1, 3)

    def outer(k):
        return pl.ds(pl.multiple_of(base + lax.rem(first + k, 4) * 128, 128), 128)

    def inner(k):
        return pl.ds(pl.multiple_of(base + first * 128 + lax.rem(second + k, 4) * 32, 32), 32)

    copies = [wires.remote(part.at[outer(k)], land.at[pl.ds((k - 1) * 128, 128)], first_ids[k]) for k in order]
    yield
    for copy in copies:
        copy.wait_recv()
    part[outer(0)] = add(part[outer(0)], land[0:128], land[128:256], land[256:384]).astype(BF16)
    copies = [wires.remote(part.at[inner(k)], land.at[pl.ds(352 + k * 32, 32)], second_ids[k]) for k in order]
    yield
    for copy in copies:
        copy.wait_recv()
    cent[inner(0)] = finish(add(part[inner(0)], land[384:416], land[416:448], land[448:480]))
    copies = [wires.remote(cent.at[inner(0)], cent.at[inner(0)], second_ids[k]) for k in order]
    yield
    for copy in copies:
        copy.wait_recv()
    copies = [wires.remote(cent.at[outer(0)], cent.at[outer(0)], first_ids[k]) for k in order]
    yield
    for copy in copies:
        copy.wait_recv()
    yield


def centroid_kernel(points, labels, old, all_points, blended, pts, lab, onehot, old_rows, weights, held, *rest):
    n_groups = len(GROUPS)
    parts, lands, cents = rest[:n_groups], rest[n_groups : 2 * n_groups], rest[2 * n_groups : 3 * n_groups]
    send, recv, local = rest[3 * n_groups :]
    wires = Wires(send, recv, local)
    p, c = lax.axis_index("point"), lax.axis_index("cent")
    x, z, y, core = p // 4, lax.rem(p, 4), c // 2, lax.rem(c, 2)

    def ring(k, by):
        return lax.rem(k + 4 + by, 4)

    up, across, down = ({"cent": ring(y, by) * 2 + core} for by in (1, 2, 3))
    sibling = {"cent": y * 2 + 1 - core}
    x_ids = {by: {"point": ring(x, by) * 4 + z} for by in (1, 2, 3)}
    z_ids = {by: {"point": x * 4 + ring(z, by)} for by in (1, 2, 3)}
    partners = (up, across, down, sibling, *x_ids.values(), *z_ids.values())

    rows = points.shape[0]
    loads = [wires.here(labels, lab.at[0]), wires.here(points, pts.at[pl.ds(0, rows)])]
    row_a = pl.multiple_of(x * 128 + z * 32, 32)
    row_b = pl.multiple_of(512 + z * 128 + x * 32, 32)
    old_loads = [wires.here(old.at[pl.ds(row_a, 32)], old_rows.at[0]), wires.here(old.at[pl.ds(row_b, 32)], old_rows.at[1])]

    barrier = pltpu.get_barrier_semaphore()
    for other in partners:
        pl.semaphore_signal(barrier, inc=1, device_id=other, device_id_type=MESH)
    pl.semaphore_wait(barrier, len(partners))
    for load in loads:
        load.wait()

    n_chunks = pts.shape[1] // LANES
    gathers = []

    def start_gather(t):
        if t < n_chunks:
            buf = lambda k: pts.at[pl.ds(k * rows, rows), pl.ds(t * LANES, LANES)]
            gathers.append(gather_chunk(wires, buf, up, down, sibling))
            next(gathers[t])

    label_gather = gather_labels(wires, lab, up, down, across, sibling)
    next(label_gather)
    start_gather(0)
    start_gather(1)

    n_rows = onehot.shape[0]
    first_id = c * n_rows
    tile = 64

    def match(slots):
        @pl.loop(0, n_rows // tile)
        def _(r):
            row = pl.multiple_of(r * tile, tile)
            ids = first_id + row + lax.broadcasted_iota(jnp.int32, (tile, rows), 0)
            for k in slots:
                same = ids == lab[k, 0:1, :]
                onehot[pl.ds(row, tile), k * rows : (k + 1) * rows] = jnp.where(same, 1.0, 0.0).astype(BF16)

    width0 = GROUPS[0] * LANES

    def count_digits():
        ones = jnp.ones((onehot.shape[1], DIGITS), BF16)

        @pl.loop(0, n_rows // 256)
        def _(r):
            row = pl.ds(pl.multiple_of(r * 256, 256), 256)
            count = jnp.dot(onehot[row, :], ones, preferred_element_type=F32).astype(jnp.int32)
            place = lax.broadcasted_iota(jnp.int32, count.shape, 1) & 3
            digit = lax.shift_right_logical(count, place * 4) & 15
            parts[0][row, width0:] = digit.astype(F32).astype(BF16)

    def finisher(g, half):
        start = sum(GROUPS[:g]) * LANES
        width = GROUPS[g] * LANES

        def finish(total):
            if g == 0:
                place = lax.broadcasted_iota(jnp.int32, (32, DIGITS), 1)
                scale = jnp.where(place == 0, 1.0, jnp.where(place == 1, 16.0, jnp.where(place == 2, 256.0, 4096.0)))
                digits = jnp.where(place < 4, total[:, width:] * scale, 0.0)
                count = jnp.sum(digits, axis=1, keepdims=True)
                weights[half, 0] = jnp.broadcast_to(jnp.where(count > 0.0, 0.5 / jnp.maximum(count, 1.0), 0.0), (32, 128))
                weights[half, 1] = jnp.broadcast_to(jnp.where(count > 0.0, 0.5, 1.0), (32, 128))
            new_w, old_w = weights[half, 0][:, 0:1], weights[half, 1][:, 0:1]
            old_part = old_rows[half, :, start : start + width].astype(F32)
            return (total[:, :width] * new_w + old_part * old_w).astype(BF16)

        return finish

    flying = []

    near_rows = 6 * rows

    def sum_near(g):
        start, width = sum(GROUPS[:g]) * LANES, GROUPS[g] * LANES

        @pl.loop(0, n_rows // 256)
        def _(r):
            row = pl.ds(pl.multiple_of(r * 256, 256), 256)
            held[row, 0:width] = jnp.dot(
                onehot[row, 0:near_rows], pts[0:near_rows, start : start + width], preferred_element_type=F32
            )

    def start_group(g, split):
        start, width = sum(GROUPS[:g]) * LANES, GROUPS[g] * LANES
        part = parts[g]

        @pl.loop(0, n_rows // 256)
        def _(r):
            row = pl.ds(pl.multiple_of(r * 256, 256), 256)
            if split:
                sums = held[row, 0:width] + jnp.dot(
                    onehot[row, near_rows:], pts[near_rows:, start : start + width], preferred_element_type=F32
                )
            else:
                sums = jnp.dot(onehot[row, :], pts[:, start : start + width], preferred_element_type=F32)
            part[row, 0:width] = sums.astype(BF16)

        halves = (
            reduce_half(wires, 0, x, z, x_ids, z_ids, part, lands[g].at[0], cents[g], finisher(g, 0)),
            reduce_half(wires, 512, z, x, z_ids, x_ids, part, lands[g].at[1], cents[g], finisher(g, 1)),
        )
        for half in halves:
            next(half)
        flying.append((g, halves))

    stores, steps = [], [0] * n_groups

    def advance():
        for entry in list(flying):
            g, halves = entry
            for half in halves:
                next(half)
            steps[g] += 1
            if steps[g] == 4:
                flying.remove(entry)
                start, width = sum(GROUPS[:g]) * LANES, GROUPS[g] * LANES
                stores.append(wires.here(cents[g], blended.at[:, pl.ds(start, width)]))

    def store_points(t):
        lanes = pl.ds(t * LANES, LANES)
        stores.append(wires.here(pts.at[:, lanes], all_points.at[:, lanes]))

    def complete(t):
        next(gathers[t])
        store_points(t)
        if t + 1 in ends:
            start_group(ends.index(t + 1), False)

    ends = [sum(GROUPS[: g + 1]) for g in range(n_groups)]
    next(label_gather)
    for t in range(n_chunks):
        next(gathers[t])
        start_gather(t + 2)
        advance()
        if t == 0:
            next(label_gather)
            match(range(4))
        if t == 1:
            match(range(4, 8))
        if t == 2:
            count_digits()
            for load in old_loads:
                load.wait()
        if t >= 1:
            next(gathers[t - 1])
            next(gathers[t - 1])
        if t >= 2:
            complete(t - 2)
    last = n_chunks - 1
    complete(last - 1)
    next(gathers[last])
    sum_near(n_groups - 1)
    next(gathers[last])
    next(gathers[last])
    start_group(n_groups - 1, True)
    store_points(last)
    while flying:
        advance()
    for copy in wires.sent:
        copy.wait_send()
    for copy in stores:
        copy.wait()


def distance_kernel(points, blended, new, out, cent_sq):
    @pl.when(pl.program_id(0) == 0)
    def _():
        ones = jnp.ones((8, blended.shape[1]), BF16)
        tile = 128

        for r in range(blended.shape[0] // tile):
            row = pl.ds(r * tile, tile)
            wide = blended[row, :].astype(F32)
            scale = lax.rsqrt(jnp.sum(wide * wide, axis=1, keepdims=True) + 1e-06)
            rounded = (wide * scale).astype(BF16)
            new[row, :] = rounded
            square = jnp.square(rounded.astype(F32))
            high = square.astype(BF16)
            low = (square - high.astype(F32)).astype(BF16)
            nt = (((1,), (1,)), ((), ()))
            cent_sq[:, r * tile : (r + 1) * tile] = lax.dot_general(
                ones, high, nt, preferred_element_type=F32
            ) + lax.dot_general(ones, low, nt, preferred_element_type=F32)

    block = points[...]
    wide = block.astype(F32)
    point_sq = jnp.sum(wide * wide, axis=1, keepdims=True)
    products = lax.dot_general(block, new[...], (((1,), (1,)), ((), ())), preferred_element_type=F32)
    out[...] = (point_sq + cent_sq[0:1, :]) - 2.0 * products


def block_of(k):
    c = lax.axis_index("cent")
    y, core = c // 2, lax.rem(c, 2)
    near = lax.rem(k, 3)
    shift = jnp.where(k >= 6, 2, jnp.where(near == 1, 3, jnp.where(near == 2, 1, 0)))
    sibling = (k == 7) | ((k >= 3) & (k < 6))
    return lax.rem(y + shift, 4) * 2 + jnp.where(sibling, 1 - core, core)


def shards(points, assign, old_centroids):
    rows, width = points.shape
    n_rows = old_centroids.shape[0]
    labels = jnp.broadcast_to(assign[None, :], (8, rows))
    group = 8 * rows
    widths = [n * LANES for n in GROUPS]
    sums = [w + (DIGITS if g == 0 else 0) for g, w in enumerate(widths)]
    n_remote = 9 * (width // LANES) + 7 + 24 * len(GROUPS)
    everywhere = pl.BlockSpec(memory_space=pl.ANY)
    all_points, blended = pl.pallas_call(
        centroid_kernel,
        out_shape=(jax.ShapeDtypeStruct((group, width), BF16), jax.ShapeDtypeStruct((n_rows, width), BF16)),
        in_specs=[everywhere] * 3,
        out_specs=(everywhere, everywhere),
        scratch_shapes=[
            pltpu.VMEM((group, width), BF16),
            pltpu.VMEM((8, 8, rows), jnp.int32),
            pltpu.VMEM((n_rows, group), BF16),
            pltpu.VMEM((2, 32, width), BF16),
            pltpu.VMEM((2, 2, 32, 128), F32),
            pltpu.VMEM((n_rows, GROUPS[-1] * LANES), F32),
            *[pltpu.VMEM((n_rows, w), BF16) for w in sums],
            *[pltpu.VMEM((2, 480, w), BF16) for w in sums],
            *[pltpu.VMEM((n_rows, w), BF16) for w in widths],
            pltpu.SemaphoreType.DMA((n_remote,)),
            pltpu.SemaphoreType.DMA((n_remote,)),
            pltpu.SemaphoreType.DMA((4 + width // LANES + len(GROUPS),)),
        ],
        compiler_params=pltpu.CompilerParams(
            collective_id=0, has_side_effects=True, vmem_limit_bytes=40 * 2**20
        ),
        cost_estimate=pl.CostEstimate(flops=2 * n_rows * group * width, bytes_accessed=2 * group * width, transcendentals=0),
    )(*(pltpu.with_memory_space_constraint(a, pltpu.HBM) for a in (points, labels, old_centroids)))
    new_centroids, distances = pl.pallas_call(
        distance_kernel,
        grid=(8,),
        out_shape=(jax.ShapeDtypeStruct((n_rows, width), BF16), jax.ShapeDtypeStruct((group, n_rows), F32)),
        in_specs=[
            pl.BlockSpec((rows, width), lambda k: (k, 0)),
            pl.BlockSpec((n_rows, width), lambda k: (0, 0)),
        ],
        out_specs=(
            pl.BlockSpec((n_rows, width), lambda k: (0, 0)),
            pl.BlockSpec((rows, n_rows), lambda k: (block_of(k), 0)),
        ),
        scratch_shapes=[pltpu.VMEM((8, n_rows), F32)],
        compiler_params=pltpu.CompilerParams(vmem_limit_bytes=40 * 2**20),
        cost_estimate=pl.CostEstimate(
            flops=2 * n_rows * group * width, bytes_accessed=4 * group * n_rows + 2 * group * width, transcendentals=0
        ),
    )(all_points, blended)
    return new_centroids, distances


def solution(mesh):
    return jax.shard_map(
        shards,
        mesh=mesh,
        in_specs=(P(("point", "cent"), None), P(("point", "cent")), P("cent", None)),
        out_specs=(P("cent", None), P("point", "cent")),
        check_vma=False,
    )
```

```python
import functools

import jax
import jax.numpy as jnp
from jax import lax
from jax.experimental import pallas as pl
from jax.experimental.pallas import tpu as pltpu
from jax.sharding import PartitionSpec as P

MESH = pl.DeviceIdType.MESH
F32, BF16 = jnp.float32, jnp.bfloat16
LANES = 256
DIGITS = 128


class Wires:
    def __init__(self, send, recv, local):
        self.send, self.recv, self.local = send, recv, local
        self.n_remote = self.n_local = 0
        self.sent, self.stored = [], []

    def remote(self, src, dst, target):
        index = self.n_remote
        self.n_remote += 1
        copy = pltpu.make_async_remote_copy(
            src_ref=src, dst_ref=dst, send_sem=self.send.at[index], recv_sem=self.recv.at[index],
            device_id=target, device_id_type=MESH,
        )
        copy.start()
        self.sent.append(copy)
        return copy

    def here(self, src, dst):
        copy = pltpu.make_async_copy(src, dst, self.local.at[self.n_local])
        self.n_local += 1
        copy.start()
        return copy


def gather_chunk(wires, block, rows, up, down, sibling):
    half = rows // 2
    from_below = wires.remote(block(0, rows), block(rows, rows), up)
    from_above = wires.remote(block(0, rows), block(2 * rows, rows), down)
    yield
    from_below.wait_recv()
    far_a = wires.remote(block(rows, half), block(6 * rows, half), up)
    from_above.wait_recv()
    far_b = wires.remote(block(2 * rows + half, half), block(6 * rows + half, half), down)
    near = wires.remote(block(0, 3 * rows), block(3 * rows, 3 * rows), sibling)
    yield
    near.wait_recv()
    yield
    far_a.wait_recv()
    far_b.wait_recv()
    far = wires.remote(block(6 * rows, rows), block(7 * rows, rows), sibling)
    yield
    far.wait_recv()
    yield


def gather_labels(wires, lab, up, down, across, sibling):
    first = [wires.remote(lab.at[0], lab.at[k], target) for k, target in ((6, across), (1, up), (2, down))]
    near = [wires.remote(lab.at[0], lab.at[3], sibling)]
    yield
    for copy, k, to in zip(first[1:] + first[:1], (1, 2, 6), (4, 5, 7)):
        copy.wait_recv()
        near.append(wires.remote(lab.at[k], lab.at[to], sibling))
    yield
    for copy in near:
        copy.wait_recv()
    yield


def add(*terms):
    total = terms[0].astype(F32)
    for term in terms[1:]:
        total = total + term.astype(F32)
    return total


def reduce_half(wires, base, first, second, first_ids, second_ids, part, land, cent, finish):
    order = (2, 1, 3)

    def outer(k):
        return pl.ds(pl.multiple_of(base + lax.rem(first + k, 4) * 128, 128), 128)

    def inner(k):
        return pl.ds(pl.multiple_of(base + first * 128 + lax.rem(second + k, 4) * 32, 32), 32)

    copies = [wires.remote(part.at[outer(k)], land.at[pl.ds((k - 1) * 128, 128)], first_ids[k]) for k in order]
    yield
    for copy in copies:
        copy.wait_recv()
    part[outer(0)] = add(part[outer(0)], land[0:128], land[128:256], land[256:384]).astype(BF16)
    copies = [wires.remote(part.at[inner(k)], land.at[pl.ds(352 + k * 32, 32)], second_ids[k]) for k in order]
    yield
    for copy in copies:
        copy.wait_recv()
    cent[inner(0)] = finish(add(part[inner(0)], land[384:416], land[416:448], land[448:480]))
    copies = [wires.remote(cent.at[inner(0)], cent.at[inner(0)], second_ids[k]) for k in order]
    yield
    for copy in copies:
        copy.wait_recv()
    copies = [wires.remote(cent.at[outer(0)], cent.at[outer(0)], first_ids[k]) for k in order]
    yield
    for copy in copies:
        copy.wait_recv()
    yield


def centroid_kernel(points, labels, old, all_points, blended, pts, lab, onehot, old_rows, weights, held, *rest):
    n_groups = len(rest) // 3 - 1
    parts, lands, cents = rest[:n_groups], rest[n_groups : 2 * n_groups], rest[2 * n_groups : 3 * n_groups]
    send, recv, local = rest[3 * n_groups :]
    wires = Wires(send, recv, local)
    p, c = lax.axis_index("point"), lax.axis_index("cent")
    x, z, y, core = p // 4, lax.rem(p, 4), c // 2, lax.rem(c, 2)

    def ring(k, by):
        return lax.rem(k + 4 + by, 4)

    up, across, down = ({"cent": ring(y, by) * 2 + core} for by in (1, 2, 3))
    sibling = {"cent": y * 2 + 1 - core}
    x_ids = {by: {"point": ring(x, by) * 4 + z} for by in (1, 2, 3)}
    z_ids = {by: {"point": x * 4 + ring(z, by)} for by in (1, 2, 3)}
    partners = (up, across, down, sibling, *x_ids.values(), *z_ids.values())

    rows = points.shape[0]
    loads = [wires.here(labels, lab.at[0]), wires.here(points, pts.at[pl.ds(0, rows)])]
    row_a = pl.multiple_of(x * 128 + z * 32, 32)
    row_b = pl.multiple_of(512 + z * 128 + x * 32, 32)
    old_loads = [wires.here(old.at[pl.ds(row_a, 32)], old_rows.at[0]), wires.here(old.at[pl.ds(row_b, 32)], old_rows.at[1])]

    barrier = pltpu.get_barrier_semaphore()
    for other in partners:
        pl.semaphore_signal(barrier, inc=1, device_id=other, device_id_type=MESH)
    pl.semaphore_wait(barrier, len(partners))
    for load in loads:
        load.wait()

    n_chunks = pts.shape[1] // LANES
    gathers = []

    def start_gather(t):
        if t < n_chunks:
            block = lambda row, count: pts.at[pl.ds(row, count), pl.ds(t * LANES, LANES)]
            gathers.append(gather_chunk(wires, block, rows, up, down, sibling))
            next(gathers[t])

    label_gather = gather_labels(wires, lab, up, down, across, sibling)
    next(label_gather)
    start_gather(0)
    start_gather(1)

    n_rows = onehot.shape[0]
    first_id = c * n_rows
    tile = 64

    def match(slots):
        @pl.loop(0, n_rows // tile)
        def _(r):
            row = pl.multiple_of(r * tile, tile)
            ids = first_id + row + lax.broadcasted_iota(jnp.int32, (tile, rows), 0)
            for k in slots:
                same = ids == lab[k, 0:1, :]
                onehot[pl.ds(row, tile), k * rows : (k + 1) * rows] = jnp.where(same, 1.0, 0.0).astype(BF16)

    def count_digits():
        ones = jnp.ones((onehot.shape[1], DIGITS), BF16)

        @pl.loop(0, n_rows // 256)
        def _(r):
            row = pl.ds(pl.multiple_of(r * 256, 256), 256)
            count = jnp.dot(onehot[row, :], ones, preferred_element_type=F32).astype(jnp.int32)
            place = lax.broadcasted_iota(jnp.int32, count.shape, 1) & 3
            digit = lax.shift_right_logical(count, place * 4) & 15
            parts[0][row, LANES:] = digit.astype(F32).astype(BF16)

    def finisher(g, half):
        start, width = g * LANES, LANES

        def finish(total):
            if g == 0:
                place = lax.broadcasted_iota(jnp.int32, (32, DIGITS), 1)
                scale = jnp.where(place == 0, 1.0, jnp.where(place == 1, 16.0, jnp.where(place == 2, 256.0, 4096.0)))
                digits = jnp.where(place < 4, total[:, width:] * scale, 0.0)
                count = jnp.sum(digits, axis=1, keepdims=True)
                weights[half, 0] = jnp.broadcast_to(jnp.where(count > 0.0, 0.5 / jnp.maximum(count, 1.0), 0.0), (32, 128))
                weights[half, 1] = jnp.broadcast_to(jnp.where(count > 0.0, 0.5, 1.0), (32, 128))
            new_w, old_w = weights[half, 0][:, 0:1], weights[half, 1][:, 0:1]
            old_part = old_rows[half, :, start : start + width].astype(F32)
            return (total[:, :width] * new_w + old_part * old_w).astype(BF16)

        return finish

    near_rows = 6 * rows
    halves, stores = {}, []

    def sum_near(g):
        @pl.loop(0, n_rows // 256)
        def _(r):
            row = pl.ds(pl.multiple_of(r * 256, 256), 256)
            held[row, :] = jnp.dot(
                onehot[row, 0:near_rows], pts[0:near_rows, g * LANES : (g + 1) * LANES], preferred_element_type=F32
            )

    def reduce(g, split=False):
        lanes = slice(g * LANES, (g + 1) * LANES)

        @pl.loop(0, n_rows // 256)
        def _(r):
            row = pl.ds(pl.multiple_of(r * 256, 256), 256)
            if split:
                sums = held[row, :] + jnp.dot(onehot[row, near_rows:], pts[near_rows:, lanes], preferred_element_type=F32)
            else:
                sums = jnp.dot(onehot[row, :], pts[:, lanes], preferred_element_type=F32)
            parts[g][row, 0:LANES] = sums.astype(BF16)

        halves[g] = (
            reduce_half(wires, 0, x, z, x_ids, z_ids, parts[g], lands[g].at[0], cents[g], finisher(g, 0)),
            reduce_half(wires, 512, z, x, z_ids, x_ids, parts[g], lands[g].at[1], cents[g], finisher(g, 1)),
        )
        advance(g)

    def advance(*groups):
        for g in groups:
            for half in halves[g]:
                next(half)

    def gathered(t):
        next(gathers[t])

    def store_points(t):
        lanes = pl.ds(t * LANES, LANES)
        stores.append(wires.here(pts.at[:, lanes], all_points.at[:, lanes]))

    def store_centroids(g):
        stores.append(wires.here(cents[g], blended.at[:, pl.ds(g * LANES, LANES)]))

    next(label_gather)
    next(label_gather)
    match(range(4))
    gathered(0)
    start_gather(2)
    match(range(4, 8))
    count_digits()
    for load in old_loads:
        load.wait()
    gathered(0)
    gathered(1)
    start_gather(3)
    gathered(0)
    gathered(0)
    reduce(0)
    gathered(1)
    gathered(2)
    gathered(1)
    advance(0)
    gathered(1)
    reduce(1)
    advance(0)
    gathered(2)
    gathered(2)
    gathered(3)
    advance(0)
    gathered(2)
    reduce(2)
    for t in range(3):
        store_points(t)
    advance(1)
    gathered(3)
    sum_near(3)
    gathered(3)
    advance(1)
    gathered(3)
    reduce(3, split=True)
    store_points(3)
    advance(0, 1, 2, 3)
    store_centroids(0)
    advance(1, 2, 3)
    store_centroids(1)
    advance(2, 3)
    advance(2, 3)
    store_centroids(2)
    store_centroids(3)
    for copy in wires.sent:
        copy.wait_send()
    for copy in stores:
        copy.wait()


def distance_kernel(points, blended, new, out, cent_sq):
    @pl.when(pl.program_id(0) == 0)
    def _():
        ones = jnp.ones((8, blended.shape[1]), BF16)
        tile = 128

        for r in range(blended.shape[0] // tile):
            row = pl.ds(r * tile, tile)
            wide = blended[row, :].astype(F32)
            scale = lax.rsqrt(jnp.sum(wide * wide, axis=1, keepdims=True) + 1e-06)
            rounded = (wide * scale).astype(BF16)
            new[row, :] = rounded
            square = jnp.square(rounded.astype(F32))
            high = square.astype(BF16)
            low = (square - high.astype(F32)).astype(BF16)
            nt = (((1,), (1,)), ((), ()))
            cent_sq[:, r * tile : (r + 1) * tile] = lax.dot_general(
                ones, high, nt, preferred_element_type=F32
            ) + lax.dot_general(ones, low, nt, preferred_element_type=F32)

    block = points[...]
    wide = block.astype(F32)
    point_sq = jnp.sum(wide * wide, axis=1, keepdims=True)
    products = lax.dot_general(block, new[...], (((1,), (1,)), ((), ())), preferred_element_type=F32)
    out[...] = (point_sq + cent_sq[0:1, :]) - 2.0 * products


def block_of(k):
    c = lax.axis_index("cent")
    y, core = c // 2, lax.rem(c, 2)
    near = lax.rem(k, 3)
    shift = jnp.where(k >= 6, 2, jnp.where(near == 1, 3, jnp.where(near == 2, 1, 0)))
    sibling = (k == 7) | ((k >= 3) & (k < 6))
    return lax.rem(y + shift, 4) * 2 + jnp.where(sibling, 1 - core, core)


def shards(points, assign, old_centroids):
    rows, width = points.shape
    n_rows = old_centroids.shape[0]
    labels = jnp.broadcast_to(assign[None, :], (8, rows))
    group = 8 * rows
    n_chunks = width // LANES
    sums = [LANES + (DIGITS if g == 0 else 0) for g in range(n_chunks)]
    n_remote = (6 + 24) * n_chunks + 8
    everywhere = pl.BlockSpec(memory_space=pl.ANY)
    all_points, blended = pl.pallas_call(
        centroid_kernel,
        out_shape=(jax.ShapeDtypeStruct((group, width), BF16), jax.ShapeDtypeStruct((n_rows, width), BF16)),
        in_specs=[everywhere] * 3,
        out_specs=(everywhere, everywhere),
        scratch_shapes=[
            pltpu.VMEM((group, width), BF16),
            pltpu.VMEM((8, 8, rows), jnp.int32),
            pltpu.VMEM((n_rows, group), BF16),
            pltpu.VMEM((2, 32, width), BF16),
            pltpu.VMEM((2, 2, 32, 128), F32),
            pltpu.VMEM((n_rows, LANES), F32),
            *[pltpu.VMEM((n_rows, w), BF16) for w in sums],
            *[pltpu.VMEM((2, 480, w), BF16) for w in sums],
            *[pltpu.VMEM((n_rows, LANES), BF16) for _ in sums],
            pltpu.SemaphoreType.DMA((n_remote,)),
            pltpu.SemaphoreType.DMA((n_remote,)),
            pltpu.SemaphoreType.DMA((4 + 2 * n_chunks,)),
        ],
        compiler_params=pltpu.CompilerParams(
            collective_id=0, has_side_effects=True, vmem_limit_bytes=40 * 2**20
        ),
        cost_estimate=pl.CostEstimate(flops=2 * n_rows * group * width, bytes_accessed=2 * group * width, transcendentals=0),
    )(*(pltpu.with_memory_space_constraint(a, pltpu.HBM) for a in (points, labels, old_centroids)))
    new_centroids, distances = pl.pallas_call(
        distance_kernel,
        grid=(8,),
        out_shape=(jax.ShapeDtypeStruct((n_rows, width), BF16), jax.ShapeDtypeStruct((group, n_rows), F32)),
        in_specs=[
            pl.BlockSpec((rows, width), lambda k: (k, 0)),
            pl.BlockSpec((n_rows, width), lambda k: (0, 0)),
        ],
        out_specs=(
            pl.BlockSpec((n_rows, width), lambda k: (0, 0)),
            pl.BlockSpec((rows, n_rows), lambda k: (block_of(k), 0)),
        ),
        scratch_shapes=[pltpu.VMEM((8, n_rows), F32)],
        compiler_params=pltpu.CompilerParams(vmem_limit_bytes=40 * 2**20),
        cost_estimate=pl.CostEstimate(
            flops=2 * n_rows * group * width, bytes_accessed=4 * group * n_rows + 2 * group * width, transcendentals=0
        ),
    )(all_points, blended)
    return new_centroids, distances


def solution(mesh):
    return jax.shard_map(
        shards,
        mesh=mesh,
        in_specs=(P(("point", "cent"), None), P(("point", "cent")), P("cent", None)),
        out_specs=(P("cent", None), P("point", "cent")),
        check_vma=False,
    )
```

```python
import functools

import jax
import jax.numpy as jnp
from jax import lax
from jax.experimental import pallas as pl
from jax.experimental.pallas import tpu as pltpu
from jax.sharding import PartitionSpec as P

MESH = pl.DeviceIdType.MESH
F32, BF16 = jnp.float32, jnp.bfloat16
WIDTHS = (256, 256, 256, 128, 128)
STARTS = tuple(sum(WIDTHS[:t]) for t in range(len(WIDTHS)))
DIGITS = 128


class Wires:
    def __init__(self, send, recv, local):
        self.send, self.recv, self.local = send, recv, local
        self.n_remote = self.n_local = 0
        self.sent, self.stored = [], []

    def remote(self, src, dst, target):
        index = self.n_remote
        self.n_remote += 1
        copy = pltpu.make_async_remote_copy(
            src_ref=src, dst_ref=dst, send_sem=self.send.at[index], recv_sem=self.recv.at[index],
            device_id=target, device_id_type=MESH,
        )
        copy.start()
        self.sent.append(copy)
        return copy

    def here(self, src, dst):
        copy = pltpu.make_async_copy(src, dst, self.local.at[self.n_local])
        self.n_local += 1
        copy.start()
        return copy


def gather_chunk(wires, block, rows, up, down, sibling):
    half = rows // 2
    from_below = wires.remote(block(0, rows), block(rows, rows), up)
    from_above = wires.remote(block(0, rows), block(2 * rows, rows), down)
    yield
    from_below.wait_recv()
    far_a = wires.remote(block(rows, half), block(6 * rows, half), up)
    from_above.wait_recv()
    far_b = wires.remote(block(2 * rows + half, half), block(6 * rows + half, half), down)
    near = wires.remote(block(0, 3 * rows), block(3 * rows, 3 * rows), sibling)
    yield
    near.wait_recv()
    yield
    far_a.wait_recv()
    far_b.wait_recv()
    far = wires.remote(block(6 * rows, rows), block(7 * rows, rows), sibling)
    yield
    far.wait_recv()
    yield


def gather_labels(wires, lab, up, down, across, sibling):
    first = [wires.remote(lab.at[0], lab.at[k], target) for k, target in ((6, across), (1, up), (2, down))]
    near = [wires.remote(lab.at[0], lab.at[3], sibling)]
    yield
    for copy, k, to in zip(first[1:] + first[:1], (1, 2, 6), (4, 5, 7)):
        copy.wait_recv()
        near.append(wires.remote(lab.at[k], lab.at[to], sibling))
    yield
    for copy in near:
        copy.wait_recv()
    yield


def add(*terms):
    total = terms[0].astype(F32)
    for term in terms[1:]:
        total = total + term.astype(F32)
    return total


def reduce_half(wires, base, first, second, first_ids, second_ids, part, land, cent, finish):
    order = (2, 1, 3)

    def outer(k):
        return pl.ds(pl.multiple_of(base + lax.rem(first + k, 4) * 128, 128), 128)

    def inner(k):
        return pl.ds(pl.multiple_of(base + first * 128 + lax.rem(second + k, 4) * 32, 32), 32)

    copies = [wires.remote(part.at[outer(k)], land.at[pl.ds((k - 1) * 128, 128)], first_ids[k]) for k in order]
    yield
    for copy in copies:
        copy.wait_recv()
    part[outer(0)] = add(part[outer(0)], land[0:128], land[128:256], land[256:384]).astype(BF16)
    copies = [wires.remote(part.at[inner(k)], land.at[pl.ds(352 + k * 32, 32)], second_ids[k]) for k in order]
    yield
    for copy in copies:
        copy.wait_recv()
    cent[inner(0)] = finish(add(part[inner(0)], land[384:416], land[416:448], land[448:480]))
    copies = [wires.remote(cent.at[inner(0)], cent.at[inner(0)], second_ids[k]) for k in order]
    yield
    for copy in copies:
        copy.wait_recv()
    copies = [wires.remote(cent.at[outer(0)], cent.at[outer(0)], first_ids[k]) for k in order]
    yield
    for copy in copies:
        copy.wait_recv()
    yield


def centroid_kernel(points, labels, old, all_points, blended, pts, lab, onehot, old_rows, weights, *rest):
    n_chunks = len(WIDTHS)
    parts, lands, cents, helds = (rest[k * n_chunks : (k + 1) * n_chunks] for k in range(4))
    send, recv, local = rest[4 * n_chunks :]
    wires = Wires(send, recv, local)
    p, c = lax.axis_index("point"), lax.axis_index("cent")
    x, z, y, core = p // 4, lax.rem(p, 4), c // 2, lax.rem(c, 2)

    def ring(k, by):
        return lax.rem(k + 4 + by, 4)

    up, across, down = ({"cent": ring(y, by) * 2 + core} for by in (1, 2, 3))
    sibling = {"cent": y * 2 + 1 - core}
    x_ids = {by: {"point": ring(x, by) * 4 + z} for by in (1, 2, 3)}
    z_ids = {by: {"point": x * 4 + ring(z, by)} for by in (1, 2, 3)}
    partners = (up, across, down, sibling, *x_ids.values(), *z_ids.values())

    rows = points.shape[0]
    loads = [wires.here(labels, lab.at[0]), wires.here(points, pts.at[pl.ds(0, rows)])]
    row_a = pl.multiple_of(x * 128 + z * 32, 32)
    row_b = pl.multiple_of(512 + z * 128 + x * 32, 32)
    old_loads = [wires.here(old.at[pl.ds(row_a, 32)], old_rows.at[0]), wires.here(old.at[pl.ds(row_b, 32)], old_rows.at[1])]

    barrier = pltpu.get_barrier_semaphore()
    for other in partners:
        pl.semaphore_signal(barrier, inc=1, device_id=other, device_id_type=MESH)
    pl.semaphore_wait(barrier, len(partners))
    for load in loads:
        load.wait()

    gathers = []

    def start_gather(t):
        if t < n_chunks:
            block = lambda row, count: pts.at[pl.ds(row, count), pl.ds(STARTS[t], WIDTHS[t])]
            gathers.append(gather_chunk(wires, block, rows, up, down, sibling))
            next(gathers[t])

    label_gather = gather_labels(wires, lab, up, down, across, sibling)
    next(label_gather)
    start_gather(0)
    start_gather(1)

    n_rows = onehot.shape[0]
    first_id = c * n_rows
    tile = 64

    def match(slots):
        @pl.loop(0, n_rows // tile)
        def _(r):
            row = pl.multiple_of(r * tile, tile)
            ids = first_id + row + lax.broadcasted_iota(jnp.int32, (tile, rows), 0)
            for k in slots:
                same = ids == lab[k, 0:1, :]
                onehot[pl.ds(row, tile), k * rows : (k + 1) * rows] = jnp.where(same, 1.0, 0.0).astype(BF16)

    def count_digits():
        ones = jnp.ones((onehot.shape[1], DIGITS), BF16)

        @pl.loop(0, n_rows // 256)
        def _(r):
            row = pl.ds(pl.multiple_of(r * 256, 256), 256)
            count = jnp.dot(onehot[row, :], ones, preferred_element_type=F32).astype(jnp.int32)
            place = lax.broadcasted_iota(jnp.int32, count.shape, 1) & 3
            digit = lax.shift_right_logical(count, place * 4) & 15
            parts[0][row, WIDTHS[0] :] = digit.astype(F32).astype(BF16)

    def finisher(g, half):
        start, width = STARTS[g], WIDTHS[g]

        def finish(total):
            if g == 0:
                place = lax.broadcasted_iota(jnp.int32, (32, DIGITS), 1)
                scale = jnp.where(place == 0, 1.0, jnp.where(place == 1, 16.0, jnp.where(place == 2, 256.0, 4096.0)))
                digits = jnp.where(place < 4, total[:, width:] * scale, 0.0)
                count = jnp.sum(digits, axis=1, keepdims=True)
                weights[half, 0] = jnp.broadcast_to(jnp.where(count > 0.0, 0.5 / jnp.maximum(count, 1.0), 0.0), (32, 128))
                weights[half, 1] = jnp.broadcast_to(jnp.where(count > 0.0, 0.5, 1.0), (32, 128))
            new_w, old_w = weights[half, 0][:, 0:1], weights[half, 1][:, 0:1]
            old_part = old_rows[half, :, start : start + width].astype(F32)
            return (total[:, :width] * new_w + old_part * old_w).astype(BF16)

        return finish

    near_rows = 6 * rows
    halves, stores = {}, []

    def sum_near(g):
        lanes = slice(STARTS[g], STARTS[g] + WIDTHS[g])

        @pl.loop(0, n_rows // 256)
        def _(r):
            row = pl.ds(pl.multiple_of(r * 256, 256), 256)
            helds[g][row, :] = jnp.dot(onehot[row, 0:near_rows], pts[0:near_rows, lanes], preferred_element_type=F32)

    def reduce(g):
        lanes = slice(STARTS[g], STARTS[g] + WIDTHS[g])

        @pl.loop(0, n_rows // 256)
        def _(r):
            row = pl.ds(pl.multiple_of(r * 256, 256), 256)
            sums = jnp.dot(onehot[row, near_rows:], pts[near_rows:, lanes], preferred_element_type=F32)
            parts[g][row, 0 : WIDTHS[g]] = (helds[g][row, :] + sums).astype(BF16)

        halves[g] = (
            reduce_half(wires, 0, x, z, x_ids, z_ids, parts[g], lands[g].at[0], cents[g], finisher(g, 0)),
            reduce_half(wires, 512, z, x, z_ids, x_ids, parts[g], lands[g].at[1], cents[g], finisher(g, 1)),
        )
        advance(g)

    def advance(*groups):
        for g in groups:
            for half in halves[g]:
                next(half)

    def gathered(t):
        next(gathers[t])

    def store_points(t):
        lanes = pl.ds(STARTS[t], WIDTHS[t])
        stores.append(wires.here(pts.at[:, lanes], all_points.at[:, lanes]))

    def store_centroids(g):
        stores.append(wires.here(cents[g], blended.at[:, pl.ds(STARTS[g], WIDTHS[g])]))

    next(label_gather)
    next(label_gather)
    match(range(4))
    gathered(0)
    start_gather(2)
    match(range(4, 8))
    gathered(0)
    sum_near(0)
    gathered(1)
    start_gather(3)
    count_digits()
    for load in old_loads:
        load.wait()
    gathered(0)
    gathered(1)
    sum_near(1)
    gathered(0)
    reduce(0)
    store_points(0)
    gathered(2)
    start_gather(4)
    gathered(1)
    gathered(2)
    sum_near(2)
    advance(0)
    gathered(3)
    gathered(1)
    reduce(1)
    store_points(1)
    gathered(3)
    sum_near(3)
    gathered(2)
    advance(0)
    gathered(4)
    gathered(2)
    reduce(2)
    store_points(2)
    advance(0)
    gathered(3)
    gathered(4)
    sum_near(4)
    advance(1)
    gathered(4)
    gathered(3)
    reduce(3)
    gathered(4)
    reduce(4)
    store_points(3)
    store_points(4)
    advance(0)
    store_centroids(0)
    advance(1, 2, 3, 4)
    advance(1, 2, 3, 4)
    advance(1, 2, 3, 4)
    store_centroids(1)
    advance(2, 3, 4)
    for g in (2, 3, 4):
        store_centroids(g)
    for copy in wires.sent:
        copy.wait_send()
    for copy in stores:
        copy.wait()


def distance_kernel(points, blended, new, out, cent_sq):
    @pl.when(pl.program_id(0) == 0)
    def _():
        ones = jnp.ones((8, blended.shape[1]), BF16)
        tile = 128

        for r in range(blended.shape[0] // tile):
            row = pl.ds(r * tile, tile)
            wide = blended[row, :].astype(F32)
            scale = lax.rsqrt(jnp.sum(wide * wide, axis=1, keepdims=True) + 1e-06)
            rounded = (wide * scale).astype(BF16)
            new[row, :] = rounded
            square = jnp.square(rounded.astype(F32))
            high = square.astype(BF16)
            low = (square - high.astype(F32)).astype(BF16)
            nt = (((1,), (1,)), ((), ()))
            cent_sq[:, r * tile : (r + 1) * tile] = lax.dot_general(
                ones, high, nt, preferred_element_type=F32
            ) + lax.dot_general(ones, low, nt, preferred_element_type=F32)

    block = points[...]
    wide = block.astype(F32)
    point_sq = jnp.sum(wide * wide, axis=1, keepdims=True)
    products = lax.dot_general(block, new[...], (((1,), (1,)), ((), ())), preferred_element_type=F32)
    out[...] = (point_sq + cent_sq[0:1, :]) - 2.0 * products


def block_of(k):
    c = lax.axis_index("cent")
    y, core = c // 2, lax.rem(c, 2)
    near = lax.rem(k, 3)
    shift = jnp.where(k >= 6, 2, jnp.where(near == 1, 3, jnp.where(near == 2, 1, 0)))
    sibling = (k == 7) | ((k >= 3) & (k < 6))
    return lax.rem(y + shift, 4) * 2 + jnp.where(sibling, 1 - core, core)


def shards(points, assign, old_centroids):
    rows, width = points.shape
    n_rows = old_centroids.shape[0]
    labels = jnp.broadcast_to(assign[None, :], (8, rows))
    group = 8 * rows
    n_chunks = len(WIDTHS)
    sums = [w + (DIGITS if g == 0 else 0) for g, w in enumerate(WIDTHS)]
    n_remote = (6 + 24) * n_chunks + 8
    everywhere = pl.BlockSpec(memory_space=pl.ANY)
    all_points, blended = pl.pallas_call(
        centroid_kernel,
        out_shape=(jax.ShapeDtypeStruct((group, width), BF16), jax.ShapeDtypeStruct((n_rows, width), BF16)),
        in_specs=[everywhere] * 3,
        out_specs=(everywhere, everywhere),
        scratch_shapes=[
            pltpu.VMEM((group, width), BF16),
            pltpu.VMEM((8, 8, rows), jnp.int32),
            pltpu.VMEM((n_rows, group), BF16),
            pltpu.VMEM((2, 32, width), BF16),
            pltpu.VMEM((2, 2, 32, 128), F32),
            *[pltpu.VMEM((n_rows, w), BF16) for w in sums],
            *[pltpu.VMEM((2, 480, w), BF16) for w in sums],
            *[pltpu.VMEM((n_rows, w), BF16) for w in WIDTHS],
            *[pltpu.VMEM((n_rows, w), F32) for w in WIDTHS],
            pltpu.SemaphoreType.DMA((n_remote,)),
            pltpu.SemaphoreType.DMA((n_remote,)),
            pltpu.SemaphoreType.DMA((4 + 2 * n_chunks,)),
        ],
        compiler_params=pltpu.CompilerParams(
            collective_id=0, has_side_effects=True, vmem_limit_bytes=40 * 2**20
        ),
        cost_estimate=pl.CostEstimate(flops=2 * n_rows * group * width, bytes_accessed=2 * group * width, transcendentals=0),
    )(*(pltpu.with_memory_space_constraint(a, pltpu.HBM) for a in (points, labels, old_centroids)))
    new_centroids, distances = pl.pallas_call(
        distance_kernel,
        grid=(8,),
        out_shape=(jax.ShapeDtypeStruct((n_rows, width), BF16), jax.ShapeDtypeStruct((group, n_rows), F32)),
        in_specs=[
            pl.BlockSpec((rows, width), lambda k: (k, 0)),
            pl.BlockSpec((n_rows, width), lambda k: (0, 0)),
        ],
        out_specs=(
            pl.BlockSpec((n_rows, width), lambda k: (0, 0)),
            pl.BlockSpec((rows, n_rows), lambda k: (block_of(k), 0)),
        ),
        scratch_shapes=[pltpu.VMEM((8, n_rows), F32)],
        compiler_params=pltpu.CompilerParams(vmem_limit_bytes=40 * 2**20),
        cost_estimate=pl.CostEstimate(
            flops=2 * n_rows * group * width, bytes_accessed=4 * group * n_rows + 2 * group * width, transcendentals=0
        ),
    )(all_points, blended)
    return new_centroids, distances


def solution(mesh):
    return jax.shard_map(
        shards,
        mesh=mesh,
        in_specs=(P(("point", "cent"), None), P(("point", "cent")), P("cent", None)),
        out_specs=(P("cent", None), P("point", "cent")),
        check_vma=False,
    )
```

```python
import functools

import jax
import jax.numpy as jnp
from jax import lax
from jax.experimental import pallas as pl
from jax.experimental.pallas import tpu as pltpu
from jax.sharding import PartitionSpec as P

MESH = pl.DeviceIdType.MESH
F32, BF16 = jnp.float32, jnp.bfloat16
NT = (((1,), (1,)), ((), ()))
WIDTHS = (256, 256, 256, 256)
STARTS = tuple(sum(WIDTHS[:t]) for t in range(len(WIDTHS)))
GROUPS = ((0,), (1,), (2,), (3,))
SPANS = tuple((STARTS[g[0]], sum(WIDTHS[t] for t in g)) for g in GROUPS)
ROUTES = ((("x", 0, 32), ("z", 32, 32)),) * 4
EARLY = 512
DIGITS = 128


class Wires:
    def __init__(self, send, recv, local):
        self.send, self.recv, self.local = send, recv, local
        self.n_remote = self.n_local = 0
        self.sent = []

    def remote(self, src, dst, target):
        index = self.n_remote
        self.n_remote += 1
        copy = pltpu.make_async_remote_copy(
            src_ref=src, dst_ref=dst, send_sem=self.send.at[index], recv_sem=self.recv.at[index],
            device_id=target, device_id_type=MESH,
        )
        copy.start()
        self.sent.append(copy)
        return copy

    def settle(self, keep=0):
        count = max(len(self.sent) - keep, 0)
        for copy in self.sent[:count]:
            copy.wait_send()
        del self.sent[:count]

    def here(self, src, dst):
        copy = pltpu.make_async_copy(src, dst, self.local.at[self.n_local])
        self.n_local += 1
        copy.start()
        return copy


def gather_chunk(wires, block, rows, up, down, sibling):
    half = rows // 2
    from_below = wires.remote(block(0, rows), block(rows, rows), up)
    from_above = wires.remote(block(0, rows), block(2 * rows, rows), down)
    yield
    from_below.wait_recv()
    far_a = wires.remote(block(rows, half), block(6 * rows, half), up)
    from_above.wait_recv()
    far_b = wires.remote(block(2 * rows + half, half), block(6 * rows + half, half), down)
    near = wires.remote(block(0, 3 * rows), block(3 * rows, 3 * rows), sibling)
    yield
    near.wait_recv()
    yield
    far_a.wait_recv()
    far_b.wait_recv()
    far = wires.remote(block(6 * rows, rows), block(7 * rows, rows), sibling)
    yield
    far.wait_recv()
    yield


def gather_labels(wires, lab, up, down, across, sibling):
    first = [wires.remote(lab.at[0], lab.at[k], target) for k, target in ((6, across), (1, up), (2, down))]
    near = [wires.remote(lab.at[0], lab.at[3], sibling)]
    yield
    for copy, k, to in zip(first[1:] + first[:1], (1, 2, 6), (4, 5, 7)):
        copy.wait_recv()
        near.append(wires.remote(lab.at[k], lab.at[to], sibling))
    yield
    for copy in near:
        copy.wait_recv()
    yield


def add(*terms):
    total = terms[0].astype(F32)
    for term in terms[1:]:
        total = total + term.astype(F32)
    return total


def reduce_rows(wires, x_first, low, size, x, z, x_ids, z_ids, part, cent, land, land_two, finish):
    order = (2, 1, 3)
    rows = pl.ds(low, size)
    first_ids, second_ids = (x_ids, z_ids) if x_first else (z_ids, x_ids)

    def block(k):
        return (lax.rem(x + k, 4), slice(None), rows) if x_first else (slice(None), lax.rem(z + k, 4), rows)

    def cell(k):
        return (x, lax.rem(z + k, 4), rows) if x_first else (lax.rem(x + k, 4), z, rows)

    copies = [wires.remote(part.at[block(k)], land.at[k - 1], first_ids[k]) for k in order]
    yield
    for copy in copies:
        copy.wait_recv()
    part[block(0)] = add(part[block(0)], land[0], land[1], land[2]).astype(BF16)
    copies = [wires.remote(part.at[cell(k)], land_two.at[k - 1], second_ids[k]) for k in order]
    yield
    for copy in copies:
        copy.wait_recv()
    cent[cell(0)] = finish(add(part[cell(0)], land_two[0], land_two[1], land_two[2]))
    copies = [wires.remote(cent.at[cell(0)], cent.at[cell(0)], second_ids[k]) for k in order]
    yield
    for copy in copies:
        copy.wait_recv()
    copies = [wires.remote(cent.at[block(0)], cent.at[block(0)], first_ids[k]) for k in order]
    yield
    for copy in copies:
        copy.wait_recv()
    yield


def centroid_kernel(points, labels, old, products_a, products_b, products_c, products_d, late_points, blended, point_sq, pts, lab, onehot, old_rows, weights, cents, *rest):
    n_chunks, n_groups = len(WIDTHS), len(GROUPS)
    n_routes = sum(len(routes) for routes in ROUTES)
    parts, rest = rest[:n_groups], rest[n_groups:]
    lands, lands_two, rest = rest[:n_routes], rest[n_routes : 2 * n_routes], rest[2 * n_routes :]
    held_a, held_b, send, recv, local = rest
    helds = [(held_a, held_b)[t % 2].at[:, pl.ds(0, w)] for t, w in enumerate(WIDTHS)]
    wires = Wires(send, recv, local)
    p, c = lax.axis_index("point"), lax.axis_index("cent")
    x, z, y, core = p // 4, lax.rem(p, 4), c // 2, lax.rem(c, 2)

    def ring(k, by):
        return lax.rem(k + 4 + by, 4)

    up, across, down = ({"cent": ring(y, by) * 2 + core} for by in (1, 2, 3))
    sibling = {"cent": y * 2 + 1 - core}
    x_ids = {by: {"point": ring(x, by) * 4 + z} for by in (1, 2, 3)}
    z_ids = {by: {"point": x * 4 + ring(z, by)} for by in (1, 2, 3)}
    partners = (up, across, down, sibling, *x_ids.values(), *z_ids.values())

    rows = points.shape[0]
    loads = [wires.here(labels, lab.at[0]), wires.here(points, pts.at[pl.ds(0, rows)])]
    old_load = wires.here(old.at[pl.ds(pl.multiple_of(p * 64, 64), 64)], old_rows)

    barrier = pltpu.get_barrier_semaphore()
    for other in partners:
        pl.semaphore_signal(barrier, inc=1, device_id=other, device_id_type=MESH)
    pl.semaphore_wait(barrier, len(partners))
    for load in loads:
        load.wait()

    gathers = []

    def start_gather(t):
        if t < n_chunks:
            block = lambda row, count: pts.at[pl.ds(row, count), pl.ds(STARTS[t], WIDTHS[t])]
            gathers.append(gather_chunk(wires, block, rows, up, down, sibling))
            next(gathers[t])

    label_gather = gather_labels(wires, lab, up, down, across, sibling)
    next(label_gather)
    start_gather(0)
    start_gather(1)

    n_rows = onehot.shape[0]
    first_id = c * n_rows
    tile = 64

    def match(slots):
        @pl.loop(0, n_rows // tile)
        def _(r):
            row = pl.multiple_of(r * tile, tile)
            ids = first_id + row + lax.broadcasted_iota(jnp.int32, (tile, rows), 0)
            for k in slots:
                same = ids == lab[k, 0:1, :]
                onehot[pl.ds(row, tile), k * rows : (k + 1) * rows] = jnp.where(same, 1.0, 0.0).astype(BF16)

    def count_digits():
        ones = jnp.ones((onehot.shape[1], DIGITS), BF16)

        @pl.loop(0, 4)
        def _(r):
            row = pl.ds(pl.multiple_of(r * 256, 256), 256)
            count = jnp.dot(onehot[row, :], ones, preferred_element_type=F32).astype(jnp.int32)
            place = lax.broadcasted_iota(jnp.int32, count.shape, 1) & 3
            digit = lax.shift_right_logical(count, place * 4) & 15
            parts[0][r, :, :, SPANS[0][1] :] = digit.astype(F32).astype(BF16).reshape(4, 64, DIGITS)

    def finisher(g, low, size):
        start, width = SPANS[g]
        mine = slice(low, low + size)

        def finish(total):
            if g == 0:
                place = lax.broadcasted_iota(jnp.int32, (size, DIGITS), 1)
                scale = jnp.where(place == 0, 1.0, jnp.where(place == 1, 16.0, jnp.where(place == 2, 256.0, 4096.0)))
                digits = jnp.where(place < 4, total[:, width:] * scale, 0.0)
                count = jnp.sum(digits, axis=1, keepdims=True)
                weights[0, mine] = jnp.broadcast_to(jnp.where(count > 0.0, 0.5 / jnp.maximum(count, 1.0), 0.0), (size, 128))
                weights[1, mine] = jnp.broadcast_to(jnp.where(count > 0.0, 0.5, 1.0), (size, 128))
            old_part = old_rows[mine, start : start + width].astype(F32)
            return (total[:, :width] * weights[0, mine, 0:1] + old_part * weights[1, mine, 0:1]).astype(BF16)

        return finish

    near_rows = 6 * rows
    routes_of, stores = {}, []

    def sum_near(t):
        lanes = slice(STARTS[t], STARTS[t] + WIDTHS[t])

        @pl.loop(0, n_rows // 256)
        def _(r):
            row = pl.ds(pl.multiple_of(r * 256, 256), 256)
            helds[t][row, :] = jnp.dot(onehot[row, 0:near_rows], pts[0:near_rows, lanes], preferred_element_type=F32)

    def sum_far(t):
        lanes = slice(STARTS[t], STARTS[t] + WIDTHS[t])
        g = [t in group for group in GROUPS].index(True)
        to = slice(STARTS[t] - SPANS[g][0], STARTS[t] - SPANS[g][0] + WIDTHS[t])

        @pl.loop(0, 4)
        def _(r):
            row = pl.ds(pl.multiple_of(r * 256, 256), 256)
            sums = jnp.dot(onehot[row, near_rows:], pts[near_rows:, lanes], preferred_element_type=F32)
            parts[g][r, :, :, to] = (helds[t][row, :] + sums).astype(BF16).reshape(4, 64, WIDTHS[t])

    def reduce(g):
        cent = cents.at[:, :, :, pl.ds(*SPANS[g])]
        begin = sum(len(routes) for routes in ROUTES[:g])
        routes_of[g] = [
            reduce_rows(
                wires, axis == "x", low, size, x, z, x_ids, z_ids,
                parts[g], cent, lands[begin + i], lands_two[begin + i], finisher(g, low, size),
            )
            for i, (axis, low, size) in enumerate(ROUTES[g])
        ]
        advance(g)

    def advance(*groups):
        for g in groups:
            for route in routes_of[g]:
                next(route)

    def gathered(t):
        next(gathers[t])

    def store_points(t):
        if STARTS[t] >= EARLY:
            to = pl.ds(STARTS[t] - EARLY, WIDTHS[t])
            stores.append(wires.here(pts.at[:, pl.ds(STARTS[t], WIDTHS[t])], late_points.at[:, to]))

    def store_centroids(g):
        lanes = pl.ds(*SPANS[g])
        stores.append(wires.here(cents.at[:, :, :, lanes], blended.at[:, :, :, lanes]))

    def square_points():
        @pl.loop(0, pts.shape[0] // 256)
        def _(r):
            row = pl.ds(pl.multiple_of(r * 256, 256), 256)
            wide = pts[row, :].astype(F32)
            point_sq[row, :] = jnp.broadcast_to(jnp.sum(wide * wide, axis=1, keepdims=True), (256, point_sq.shape[1]))

    def multiply_early():
        for k, products in enumerate((products_a, products_b, products_c, products_d)):

            @pl.loop(0, 2)
            def _(r):
                row = pl.ds(pl.multiple_of(2 * k * rows + r * rows, rows), rows)
                rhs = cents[:, :, :, 0:EARLY].reshape(n_rows, EARLY)
                products[pl.ds(pl.multiple_of(r * rows, rows), rows), :] = lax.dot_general(
                    pts[row, 0:EARLY], rhs, NT, preferred_element_type=F32
                )

    next(label_gather)
    next(label_gather)
    match(range(4))
    gathered(0)
    start_gather(2)
    match(range(4, 8))
    gathered(0)
    sum_near(0)
    gathered(1)
    start_gather(3)
    count_digits()
    old_load.wait()
    gathered(0)
    gathered(1)
    sum_near(1)
    gathered(0)
    sum_far(0)
    reduce(0)
    gathered(2)
    gathered(1)
    gathered(2)
    sum_near(2)
    gathered(1)
    sum_far(1)
    reduce(1)
    advance(0)
    gathered(2)
    gathered(3)
    gathered(2)
    sum_far(2)
    reduce(2)
    advance(0)
    gathered(3)
    sum_near(3)
    gathered(3)
    advance(1)
    gathered(3)
    sum_far(3)
    reduce(3)
    advance(0)
    store_points(2)
    store_points(3)
    square_points()
    advance(1)
    advance(2)
    advance(3)
    advance(0)
    store_centroids(0)
    advance(1)
    advance(2)
    advance(3)
    wires.settle(20)
    advance(2)
    advance(1)
    store_centroids(1)
    advance(3)
    wires.settle(12)
    multiply_early()
    advance(2)
    store_centroids(2)
    advance(3)
    store_centroids(3)
    wires.settle()
    for copy in stores:
        copy.wait()


def distance_kernel(products_a, products_b, products_c, products_d, points, blended, point_sq, new, out, made, rows_of, staged, sems):
    n_rows, group, block = made.shape[0], points.shape[0], staged.shape[1]
    flat = blended.reshape(n_rows, blended.shape[3])
    tile = 128
    for r in range(n_rows // tile):
        row = pl.ds(r * tile, tile)
        wide = flat[row, :].astype(F32)
        scale = lax.rsqrt(jnp.sum(wide * wide, axis=1, keepdims=True) + 1e-06)
        rounded = (wide * scale).astype(BF16)
        made[row, :] = rounded
        square = jnp.square(rounded.astype(F32))
        cent_sq = jnp.sum(square, axis=1, keepdims=True)
        lane = lax.broadcasted_iota(jnp.int32, (tile, 128), 1)
        rows_of[:, r * tile : (r + 1) * tile] = jnp.where(lane < 8, scale, cent_sq).T
    new_copy = pltpu.make_async_copy(made, new, sems.at[staged.shape[0]])
    new_copy.start()
    twice, cent_sq = 2.0 * rows_of[0:1, :], rows_of[8:9, :]

    c = lax.axis_index("cent")
    y, core = c // 2, lax.rem(c, 2)
    copies = []
    for k in range(group // block):
        shift = 2 if k >= 6 else (0, 3, 1)[k % 3]
        side = 1 - core if k in (3, 4, 5, 7) else core
        place = (lax.rem(y + shift, 4) * 2 + side) * block
        slot = k % staged.shape[0]
        if k >= staged.shape[0]:
            copies[k - staged.shape[0]].wait()
        row = slice(k * block, (k + 1) * block)
        early = (products_a, products_b, products_c, products_d)[k // 2][(k % 2) * block : (k % 2 + 1) * block, :]
        late = lax.dot_general(points[row, :], flat[:, EARLY:], NT, preferred_element_type=F32)
        staged[slot] = (point_sq[row, 0:1] + cent_sq) - twice * (early + late)
        copies.append(pltpu.make_async_copy(staged.at[slot], out.at[pl.ds(pl.multiple_of(place, block), block)], sems.at[slot]))
        copies[-1].start()
    for copy in copies[-staged.shape[0] :]:
        copy.wait()
    new_copy.wait()


def shards(points, assign, old_centroids):
    rows, width = points.shape
    n_rows = old_centroids.shape[0]
    labels = jnp.broadcast_to(assign[None, :], (8, rows))
    group = 8 * rows
    n_chunks = len(WIDTHS)
    sums = [w + (DIGITS if g == 0 else 0) for g, (_, w) in enumerate(SPANS)]
    routes = [(size, sums[g]) for g, of_group in enumerate(ROUTES) for _, _, size in of_group]
    n_remote = 6 * n_chunks + 12 * len(routes) + 8
    hbm, vmem = pl.BlockSpec(memory_space=pltpu.HBM), pl.BlockSpec(memory_space=pltpu.VMEM)
    handed_on = pl.pallas_call(
        centroid_kernel,
        out_shape=(
            *[pltpu.VMEM((group // 4, n_rows), F32)] * 4,
            pltpu.VMEM((group, width - EARLY), BF16),
            pltpu.VMEM((4, 4, 64, width), BF16),
            pltpu.VMEM((group, 128), F32),
        ),
        in_specs=[hbm] * 3,
        out_specs=(vmem,) * 7,
        scratch_shapes=[
            pltpu.VMEM((group, width), BF16),
            pltpu.VMEM((8, 8, rows), jnp.int32),
            pltpu.VMEM((n_rows, group), BF16),
            pltpu.VMEM((64, width), BF16),
            pltpu.VMEM((2, 64, 128), F32),
            pltpu.VMEM((4, 4, 64, width), BF16),
            *[pltpu.VMEM((4, 4, 64, w), BF16) for w in sums],
            *[pltpu.VMEM((3, 4, size, w), BF16) for size, w in routes],
            *[pltpu.VMEM((3, size, w), BF16) for size, w in routes],
            *[pltpu.VMEM((n_rows, max(WIDTHS)), F32)] * 2,
            pltpu.SemaphoreType.DMA((n_remote,)),
            pltpu.SemaphoreType.DMA((n_remote,)),
            pltpu.SemaphoreType.DMA((4 + 2 * n_chunks,)),
        ],
        compiler_params=pltpu.CompilerParams(
            collective_id=0, has_side_effects=True, vmem_limit_bytes=26 * 2**20
        ),
        cost_estimate=pl.CostEstimate(flops=3 * n_rows * group * width, bytes_accessed=2 * group * width, transcendentals=0),
    )(*(pltpu.with_memory_space_constraint(a, pltpu.HBM) for a in (points, labels, old_centroids)))
    new_centroids, distances = pl.pallas_call(
        distance_kernel,
        out_shape=(jax.ShapeDtypeStruct((n_rows, width), BF16), jax.ShapeDtypeStruct((group, n_rows), F32)),
        in_specs=[vmem] * 7,
        out_specs=(hbm, hbm),
        scratch_shapes=[
            pltpu.VMEM((n_rows, width), BF16),
            pltpu.VMEM((128, n_rows), F32),
            pltpu.VMEM((3, rows, n_rows), F32),
            pltpu.SemaphoreType.DMA((4,)),
        ],
        compiler_params=pltpu.CompilerParams(vmem_limit_bytes=16 * 2**20),
        cost_estimate=pl.CostEstimate(flops=n_rows * group * width, bytes_accessed=4 * group * n_rows, transcendentals=0),
    )(*(pltpu.with_memory_space_constraint(a, pltpu.VMEM) for a in handed_on))
    return new_centroids, distances


def solution(mesh):
    return jax.shard_map(
        shards,
        mesh=mesh,
        in_specs=(P(("point", "cent"), None), P(("point", "cent")), P("cent", None)),
        out_specs=(P("cent", None), P("point", "cent")),
        check_vma=False,
    )
```

```python
import functools

import jax
import jax.numpy as jnp
from jax import lax
from jax.experimental import pallas as pl
from jax.experimental.pallas import tpu as pltpu
from jax.sharding import PartitionSpec as P

MESH = pl.DeviceIdType.MESH
F32, BF16 = jnp.float32, jnp.bfloat16
NT = (((1,), (1,)), ((), ()))
WIDTHS = (256, 256, 256, 256)
STARTS = tuple(sum(WIDTHS[:t]) for t in range(len(WIDTHS)))
GROUPS = ((0,), (1,), (2,), (3,))
SPANS = tuple((STARTS[g[0]], sum(WIDTHS[t] for t in g)) for g in GROUPS)
ROUTES = ((("x", 0, 32), ("z", 32, 32)),) * 4
EARLY = 512
DIGITS = 128


class Wires:
    def __init__(self, send, recv, local):
        self.send, self.recv, self.local = send, recv, local
        self.n_remote = self.n_local = 0
        self.sent = []

    def remote(self, src, dst, target):
        index = self.n_remote
        self.n_remote += 1
        copy = pltpu.make_async_remote_copy(
            src_ref=src, dst_ref=dst, send_sem=self.send.at[index], recv_sem=self.recv.at[index],
            device_id=target, device_id_type=MESH,
        )
        copy.start()
        self.sent.append(copy)
        return copy

    def settle(self, keep=0):
        count = max(len(self.sent) - keep, 0)
        for copy in self.sent[:count]:
            copy.wait_send()
        del self.sent[:count]

    def here(self, src, dst):
        copy = pltpu.make_async_copy(src, dst, self.local.at[self.n_local])
        self.n_local += 1
        copy.start()
        return copy


def gather_chunk(wires, block, rows, up, down, sibling):
    half = rows // 2
    from_below = wires.remote(block(0, rows), block(rows, rows), up)
    from_above = wires.remote(block(0, rows), block(2 * rows, rows), down)
    yield
    from_below.wait_recv()
    far_a = wires.remote(block(rows, half), block(6 * rows, half), up)
    from_above.wait_recv()
    far_b = wires.remote(block(2 * rows + half, half), block(6 * rows + half, half), down)
    near = wires.remote(block(0, 3 * rows), block(3 * rows, 3 * rows), sibling)
    yield
    near.wait_recv()
    yield
    far_a.wait_recv()
    far_b.wait_recv()
    far = wires.remote(block(6 * rows, rows), block(7 * rows, rows), sibling)
    yield
    far.wait_recv()
    yield


def gather_labels(wires, lab, up, down, across, sibling):
    first = [wires.remote(lab.at[0], lab.at[k], target) for k, target in ((6, across), (1, up), (2, down))]
    near = [wires.remote(lab.at[0], lab.at[3], sibling)]
    yield
    for copy, k, to in zip(first[1:] + first[:1], (1, 2, 6), (4, 5, 7)):
        copy.wait_recv()
        near.append(wires.remote(lab.at[k], lab.at[to], sibling))
    yield
    for copy in near:
        copy.wait_recv()
    yield


def add(*terms):
    total = terms[0].astype(F32)
    for term in terms[1:]:
        total = total + term.astype(F32)
    return total


def reduce_rows(wires, x_first, low, size, x, z, x_ids, z_ids, part, cent, land, land_two, finish):
    order = (2, 1, 3)
    rows = pl.ds(low, size)
    first_ids, second_ids = (x_ids, z_ids) if x_first else (z_ids, x_ids)

    def block(k):
        return (lax.rem(x + k, 4), slice(None), rows) if x_first else (slice(None), lax.rem(z + k, 4), rows)

    def cell(k):
        return (x, lax.rem(z + k, 4), rows) if x_first else (lax.rem(x + k, 4), z, rows)

    copies = [wires.remote(part.at[block(k)], land.at[k - 1], first_ids[k]) for k in order]
    yield
    for copy in copies:
        copy.wait_recv()
    part[block(0)] = add(part[block(0)], land[0], land[1], land[2]).astype(BF16)
    copies = [wires.remote(part.at[cell(k)], land_two.at[k - 1], second_ids[k]) for k in order]
    yield
    for copy in copies:
        copy.wait_recv()
    cent[cell(0)] = finish(add(part[cell(0)], land_two[0], land_two[1], land_two[2]))
    copies = [wires.remote(cent.at[cell(0)], cent.at[cell(0)], second_ids[k]) for k in order]
    yield
    for copy in copies:
        copy.wait_recv()
    copies = [wires.remote(cent.at[block(0)], cent.at[block(0)], first_ids[k]) for k in order]
    yield
    for copy in copies:
        copy.wait_recv()
    yield


def centroid_kernel(points, labels, old, products_a, products_b, products_c, products_d, late_points, blended, point_sq, pts, lab, onehot, old_rows, weights, cents, *rest):
    n_chunks, n_groups = len(WIDTHS), len(GROUPS)
    n_routes = sum(len(routes) for routes in ROUTES)
    parts, rest = rest[:n_groups], rest[n_groups:]
    lands, lands_two, rest = rest[:n_routes], rest[n_routes : 2 * n_routes], rest[2 * n_routes :]
    held_a, held_b, send, recv, local = rest
    helds = [(held_a, held_b)[t % 2].at[:, pl.ds(0, w)] for t, w in enumerate(WIDTHS)]
    wires = Wires(send, recv, local)
    p, c = lax.axis_index("point"), lax.axis_index("cent")
    x, z, y, core = p // 4, lax.rem(p, 4), c // 2, lax.rem(c, 2)

    def ring(k, by):
        return lax.rem(k + 4 + by, 4)

    up, across, down = ({"cent": ring(y, by) * 2 + core} for by in (1, 2, 3))
    sibling = {"cent": y * 2 + 1 - core}
    x_ids = {by: {"point": ring(x, by) * 4 + z} for by in (1, 2, 3)}
    z_ids = {by: {"point": x * 4 + ring(z, by)} for by in (1, 2, 3)}
    partners = (up, across, down, sibling, *x_ids.values(), *z_ids.values())

    rows = points.shape[0]
    loads = [wires.here(labels, lab.at[0]), wires.here(points, pts.at[pl.ds(0, rows)])]
    old_load = wires.here(old.at[pl.ds(pl.multiple_of(p * 64, 64), 64)], old_rows)

    barrier = pltpu.get_barrier_semaphore()
    for other in partners:
        pl.semaphore_signal(barrier, inc=1, device_id=other, device_id_type=MESH)
    pl.semaphore_wait(barrier, len(partners))
    for load in loads:
        load.wait()

    gathers = []

    def start_gather(t):
        if t < n_chunks:
            block = lambda row, count: pts.at[pl.ds(row, count), pl.ds(STARTS[t], WIDTHS[t])]
            gathers.append(gather_chunk(wires, block, rows, up, down, sibling))
            next(gathers[t])

    label_gather = gather_labels(wires, lab, up, down, across, sibling)
    next(label_gather)
    start_gather(0)
    start_gather(1)

    n_rows = onehot.shape[0]
    first_id = c * n_rows
    tile = 64

    def match(slots):
        @pl.loop(0, n_rows // tile)
        def _(r):
            row = pl.multiple_of(r * tile, tile)
            ids = first_id + row + lax.broadcasted_iota(jnp.int32, (tile, rows), 0)
            for k in slots:
                same = ids == lab[k]
                onehot[pl.ds(row, tile), k * rows : (k + 1) * rows] = jnp.where(same, 1.0, 0.0).astype(BF16)

    def count_digits():
        ones = jnp.ones((onehot.shape[1], DIGITS), BF16)

        @pl.loop(0, 4)
        def _(r):
            row = pl.ds(pl.multiple_of(r * 256, 256), 256)
            count = jnp.dot(onehot[row, :], ones, preferred_element_type=F32).astype(jnp.int32)
            place = lax.broadcasted_iota(jnp.int32, count.shape, 1) & 3
            digit = lax.shift_right_logical(count, place * 4) & 15
            parts[0][r, :, :, SPANS[0][1] :] = digit.astype(F32).astype(BF16).reshape(4, 64, DIGITS)

    def finisher(g, low, size):
        start, width = SPANS[g]
        mine = slice(low, low + size)

        def finish(total):
            if g == 0:
                place = lax.broadcasted_iota(jnp.int32, (size, DIGITS), 1)
                scale = jnp.where(place == 0, 1.0, jnp.where(place == 1, 16.0, jnp.where(place == 2, 256.0, 4096.0)))
                digits = jnp.where(place < 4, total[:, width:] * scale, 0.0)
                count = jnp.sum(digits, axis=1, keepdims=True)
                weights[0, mine] = jnp.broadcast_to(jnp.where(count > 0.0, 0.5 / jnp.maximum(count, 1.0), 0.0), (size, 128))
                weights[1, mine] = jnp.broadcast_to(jnp.where(count > 0.0, 0.5, 1.0), (size, 128))
            old_part = old_rows[mine, start : start + width].astype(F32)
            return (total[:, :width] * weights[0, mine, 0:1] + old_part * weights[1, mine, 0:1]).astype(BF16)

        return finish

    near_rows = 6 * rows
    routes_of, stores = {}, []

    def sum_near(t):
        lanes = slice(STARTS[t], STARTS[t] + WIDTHS[t])

        @pl.loop(0, n_rows // 256)
        def _(r):
            row = pl.ds(pl.multiple_of(r * 256, 256), 256)
            helds[t][row, :] = jnp.dot(onehot[row, 0:near_rows], pts[0:near_rows, lanes], preferred_element_type=F32)

    def sum_far(t):
        lanes = slice(STARTS[t], STARTS[t] + WIDTHS[t])
        g = [t in group for group in GROUPS].index(True)
        to = slice(STARTS[t] - SPANS[g][0], STARTS[t] - SPANS[g][0] + WIDTHS[t])

        @pl.loop(0, 4)
        def _(r):
            row = pl.ds(pl.multiple_of(r * 256, 256), 256)
            sums = jnp.dot(onehot[row, near_rows:], pts[near_rows:, lanes], preferred_element_type=F32)
            parts[g][r, :, :, to] = (helds[t][row, :] + sums).astype(BF16).reshape(4, 64, WIDTHS[t])

    def reduce(g):
        cent = cents.at[:, :, :, pl.ds(*SPANS[g])]
        begin = sum(len(routes) for routes in ROUTES[:g])
        routes_of[g] = [
            reduce_rows(
                wires, axis == "x", low, size, x, z, x_ids, z_ids,
                parts[g], cent, lands[begin + i], lands_two[begin + i], finisher(g, low, size),
            )
            for i, (axis, low, size) in enumerate(ROUTES[g])
        ]
        advance(g)

    def advance(*groups):
        for g in groups:
            for route in routes_of[g]:
                next(route)

    def gathered(t):
        next(gathers[t])

    def store_points(t):
        if STARTS[t] >= EARLY:
            to = pl.ds(STARTS[t] - EARLY, WIDTHS[t])
            stores.append(wires.here(pts.at[:, pl.ds(STARTS[t], WIDTHS[t])], late_points.at[:, to]))

    def store_centroids(g):
        lanes = pl.ds(*SPANS[g])
        stores.append(wires.here(cents.at[:, :, :, lanes], blended.at[:, :, :, lanes]))

    def square_points():
        @pl.loop(0, pts.shape[0] // 256)
        def _(r):
            row = pl.ds(pl.multiple_of(r * 256, 256), 256)
            wide = pts[row, :].astype(F32)
            point_sq[row, :] = jnp.broadcast_to(jnp.sum(wide * wide, axis=1, keepdims=True), (256, point_sq.shape[1]))

    def multiply_early():
        for k, products in enumerate((products_a, products_b, products_c, products_d)):

            @pl.loop(0, 2)
            def _(r):
                row = pl.ds(pl.multiple_of(2 * k * rows + r * rows, rows), rows)
                rhs = cents[:, :, :, 0:EARLY].reshape(n_rows, EARLY)
                products[pl.ds(pl.multiple_of(r * rows, rows), rows), :] = lax.dot_general(
                    pts[row, 0:EARLY], rhs, NT, preferred_element_type=F32
                )

    next(label_gather)
    next(label_gather)
    match(range(4))
    gathered(0)
    start_gather(2)
    match(range(4, 8))
    gathered(0)
    sum_near(0)
    gathered(1)
    start_gather(3)
    count_digits()
    old_load.wait()
    gathered(0)
    gathered(1)
    sum_near(1)
    gathered(0)
    sum_far(0)
    reduce(0)
    gathered(2)
    gathered(1)
    gathered(2)
    sum_near(2)
    gathered(1)
    sum_far(1)
    reduce(1)
    gathered(3)
    advance(0)
    gathered(2)
    gathered(2)
    sum_far(2)
    reduce(2)
    advance(0)
    gathered(3)
    sum_near(3)
    gathered(3)
    advance(1)
    gathered(3)
    sum_far(3)
    reduce(3)
    advance(0)
    store_points(2)
    store_points(3)
    square_points()
    advance(1)
    advance(2)
    advance(3)
    advance(0)
    store_centroids(0)
    advance(1)
    advance(2)
    advance(3)
    wires.settle(20)
    advance(2)
    advance(1)
    store_centroids(1)
    advance(3)
    wires.settle(12)
    multiply_early()
    advance(2)
    store_centroids(2)
    advance(3)
    store_centroids(3)
    wires.settle()
    for copy in stores:
        copy.wait()


def distance_kernel(products_a, products_b, products_c, products_d, points, blended, point_sq, new, out, made, rows_of, staged, sems):
    n_rows, group, block = made.shape[0], points.shape[0], staged.shape[1]
    flat = blended.reshape(n_rows, blended.shape[3])
    tile = 128
    for r in range(n_rows // tile):
        row = pl.ds(r * tile, tile)
        wide = flat[row, :].astype(F32)
        scale = lax.rsqrt(jnp.sum(wide * wide, axis=1, keepdims=True) + 1e-06)
        rounded = (wide * scale).astype(BF16)
        made[row, :] = rounded
        square = jnp.square(rounded.astype(F32))
        cent_sq = jnp.sum(square, axis=1, keepdims=True)
        lane = lax.broadcasted_iota(jnp.int32, (tile, 128), 1)
        rows_of[:, r * tile : (r + 1) * tile] = jnp.where(lane < 8, scale, cent_sq).T
    new_copy = pltpu.make_async_copy(made, new, sems.at[staged.shape[0]])
    new_copy.start()
    twice, cent_sq = 2.0 * rows_of[0:1, :], rows_of[8:9, :]

    c = lax.axis_index("cent")
    y, core = c // 2, lax.rem(c, 2)
    copies = []
    for k in range(group // block):
        shift = 2 if k >= 6 else (0, 3, 1)[k % 3]
        side = 1 - core if k in (3, 4, 5, 7) else core
        place = (lax.rem(y + shift, 4) * 2 + side) * block
        slot = k % staged.shape[0]
        if k >= staged.shape[0]:
            copies[k - staged.shape[0]].wait()
        row = slice(k * block, (k + 1) * block)
        early = (products_a, products_b, products_c, products_d)[k // 2][(k % 2) * block : (k % 2 + 1) * block, :]
        late = lax.dot_general(points[row, :], flat[:, EARLY:], NT, preferred_element_type=F32)
        staged[slot] = (point_sq[row, 0:1] + cent_sq) - twice * (early + late)
        copies.append(pltpu.make_async_copy(staged.at[slot], out.at[pl.ds(pl.multiple_of(place, block), block)], sems.at[slot]))
        copies[-1].start()
    for copy in copies[-staged.shape[0] :]:
        copy.wait()
    new_copy.wait()


def shards(points, assign, old_centroids):
    rows, width = points.shape
    n_rows = old_centroids.shape[0]
    labels = assign.reshape(1, rows)
    group = 8 * rows
    n_chunks = len(WIDTHS)
    sums = [w + (DIGITS if g == 0 else 0) for g, (_, w) in enumerate(SPANS)]
    routes = [(size, sums[g]) for g, of_group in enumerate(ROUTES) for _, _, size in of_group]
    n_remote = 6 * n_chunks + 12 * len(routes) + 8
    hbm, vmem = pl.BlockSpec(memory_space=pltpu.HBM), pl.BlockSpec(memory_space=pltpu.VMEM)
    handed_on = pl.pallas_call(
        centroid_kernel,
        out_shape=(
            *[pltpu.VMEM((group // 4, n_rows), F32)] * 4,
            pltpu.VMEM((group, width - EARLY), BF16),
            pltpu.VMEM((4, 4, 64, width), BF16),
            pltpu.VMEM((group, 128), F32),
        ),
        in_specs=[hbm] * 3,
        out_specs=(vmem,) * 7,
        scratch_shapes=[
            pltpu.VMEM((group, width), BF16),
            pltpu.VMEM((8, 1, rows), jnp.int32),
            pltpu.VMEM((n_rows, group), BF16),
            pltpu.VMEM((64, width), BF16),
            pltpu.VMEM((2, 64, 128), F32),
            pltpu.VMEM((4, 4, 64, width), BF16),
            *[pltpu.VMEM((4, 4, 64, w), BF16) for w in sums],
            *[pltpu.VMEM((3, 4, size, w), BF16) for size, w in routes],
            *[pltpu.VMEM((3, size, w), BF16) for size, w in routes],
            *[pltpu.VMEM((n_rows, max(WIDTHS)), F32)] * 2,
            pltpu.SemaphoreType.DMA((n_remote,)),
            pltpu.SemaphoreType.DMA((n_remote,)),
            pltpu.SemaphoreType.DMA((4 + 2 * n_chunks,)),
        ],
        compiler_params=pltpu.CompilerParams(
            collective_id=0, has_side_effects=True, vmem_limit_bytes=26 * 2**20
        ),
        cost_estimate=pl.CostEstimate(flops=3 * n_rows * group * width, bytes_accessed=2 * group * width, transcendentals=0),
    )(*(pltpu.with_memory_space_constraint(a, pltpu.HBM) for a in (points, labels, old_centroids)))
    new_centroids, distances = pl.pallas_call(
        distance_kernel,
        out_shape=(jax.ShapeDtypeStruct((n_rows, width), BF16), jax.ShapeDtypeStruct((group, n_rows), F32)),
        in_specs=[vmem] * 7,
        out_specs=(hbm, hbm),
        scratch_shapes=[
            pltpu.VMEM((n_rows, width), BF16),
            pltpu.VMEM((128, n_rows), F32),
            pltpu.VMEM((3, rows, n_rows), F32),
            pltpu.SemaphoreType.DMA((4,)),
        ],
        compiler_params=pltpu.CompilerParams(vmem_limit_bytes=16 * 2**20),
        cost_estimate=pl.CostEstimate(flops=n_rows * group * width, bytes_accessed=4 * group * n_rows, transcendentals=0),
    )(*(pltpu.with_memory_space_constraint(a, pltpu.VMEM) for a in handed_on))
    return new_centroids, distances


def solution(mesh):
    return jax.shard_map(
        shards,
        mesh=mesh,
        in_specs=(P(("point", "cent"), None), P(("point", "cent")), P("cent", None)),
        out_specs=(P("cent", None), P("point", "cent")),
        check_vma=False,
    )
```

```python
import functools

import jax
import jax.numpy as jnp
from jax import lax
from jax.experimental import pallas as pl
from jax.experimental.pallas import tpu as pltpu
from jax.sharding import PartitionSpec as P

MESH = pl.DeviceIdType.MESH
F32, BF16 = jnp.float32, jnp.bfloat16
NT = (((1,), (1,)), ((), ()))
WIDTHS = (256, 256, 256, 256)
STARTS = tuple(sum(WIDTHS[:t]) for t in range(len(WIDTHS)))
GROUPS = ((0,), (1,), (2,), (3,))
SPANS = tuple((STARTS[g[0]], sum(WIDTHS[t] for t in g)) for g in GROUPS)
ROUTES = ((("x", 0, 32), ("z", 32, 32)),) * 4
EARLY = 512
DIGITS = 128


class Wires:
    def __init__(self, send, recv, local):
        self.send, self.recv, self.local = send, recv, local
        self.n_remote = self.n_local = 0
        self.sent = []

    def remote(self, src, dst, target):
        index = self.n_remote
        self.n_remote += 1
        copy = pltpu.make_async_remote_copy(
            src_ref=src, dst_ref=dst, send_sem=self.send.at[index], recv_sem=self.recv.at[index],
            device_id=target, device_id_type=MESH,
        )
        copy.start()
        self.sent.append(copy)
        return copy

    def settle(self, keep=0):
        count = max(len(self.sent) - keep, 0)
        for copy in self.sent[:count]:
            copy.wait_send()
        del self.sent[:count]

    def here(self, src, dst):
        copy = pltpu.make_async_copy(src, dst, self.local.at[self.n_local])
        self.n_local += 1
        copy.start()
        return copy


def gather_chunk(wires, block, rows, up, down, sibling):
    half = rows // 2
    from_below = wires.remote(block(0, rows), block(rows, rows), up)
    from_above = wires.remote(block(0, rows), block(2 * rows, rows), down)
    yield
    from_below.wait_recv()
    far_a = wires.remote(block(rows, half), block(6 * rows, half), up)
    from_above.wait_recv()
    far_b = wires.remote(block(2 * rows + half, half), block(6 * rows + half, half), down)
    near = wires.remote(block(0, 3 * rows), block(3 * rows, 3 * rows), sibling)
    yield
    near.wait_recv()
    yield
    far_a.wait_recv()
    far_b.wait_recv()
    far = wires.remote(block(6 * rows, rows), block(7 * rows, rows), sibling)
    yield
    far.wait_recv()
    yield


def gather_labels(wires, lab, up, down, across, sibling):
    first = [wires.remote(lab.at[0], lab.at[k], target) for k, target in ((6, across), (1, up), (2, down))]
    near = [wires.remote(lab.at[0], lab.at[3], sibling)]
    yield
    for copy, k, to in zip(first[1:] + first[:1], (1, 2, 6), (4, 5, 7)):
        copy.wait_recv()
        near.append(wires.remote(lab.at[k], lab.at[to], sibling))
    yield
    for copy in near:
        copy.wait_recv()
    yield


def add(*terms):
    total = terms[0].astype(F32)
    for term in terms[1:]:
        total = total + term.astype(F32)
    return total


def reduce_rows(wires, x_first, low, size, x, z, x_ids, z_ids, part, cent, land, land_two, finish):
    order = (2, 1, 3)
    rows = pl.ds(low, size)
    first_ids, second_ids = (x_ids, z_ids) if x_first else (z_ids, x_ids)

    def block(k):
        return (lax.rem(x + k, 4), slice(None), rows) if x_first else (slice(None), lax.rem(z + k, 4), rows)

    def cell(k):
        return (x, lax.rem(z + k, 4), rows) if x_first else (lax.rem(x + k, 4), z, rows)

    copies = [wires.remote(part.at[block(k)], land.at[k - 1], first_ids[k]) for k in order]
    yield
    for copy in copies:
        copy.wait_recv()
    part[block(0)] = add(part[block(0)], land[0], land[1], land[2]).astype(BF16)
    copies = [wires.remote(part.at[cell(k)], land_two.at[k - 1], second_ids[k]) for k in order]
    yield
    for copy in copies:
        copy.wait_recv()
    cent[cell(0)] = finish(add(part[cell(0)], land_two[0], land_two[1], land_two[2]))
    copies = [wires.remote(cent.at[cell(0)], cent.at[cell(0)], second_ids[k]) for k in order]
    yield
    for copy in copies:
        copy.wait_recv()
    copies = [wires.remote(cent.at[block(0)], cent.at[block(0)], first_ids[k]) for k in order]
    yield
    for copy in copies:
        copy.wait_recv()
    yield


def centroid_kernel(points, labels, old, products_a, products_b, products_c, products_d, late_points, blended, point_sq, pts, lab, onehot, old_rows, weights, cents, *rest):
    n_chunks, n_groups = len(WIDTHS), len(GROUPS)
    n_routes = sum(len(routes) for routes in ROUTES)
    parts, rest = rest[:n_groups], rest[n_groups:]
    lands, lands_two, rest = rest[:n_routes], rest[n_routes : 2 * n_routes], rest[2 * n_routes :]
    held_a, held_b, send, recv, local = rest
    helds = [(held_a, held_b)[t % 2].at[:, pl.ds(0, w)] for t, w in enumerate(WIDTHS)]
    wires = Wires(send, recv, local)
    p, c = lax.axis_index("point"), lax.axis_index("cent")
    x, z, y, core = p // 4, lax.rem(p, 4), c // 2, lax.rem(c, 2)

    def ring(k, by):
        return lax.rem(k + 4 + by, 4)

    up, across, down = ({"cent": ring(y, by) * 2 + core} for by in (1, 2, 3))
    sibling = {"cent": y * 2 + 1 - core}
    x_ids = {by: {"point": ring(x, by) * 4 + z} for by in (1, 2, 3)}
    z_ids = {by: {"point": x * 4 + ring(z, by)} for by in (1, 2, 3)}
    partners = (up, across, down, sibling, *x_ids.values(), *z_ids.values())

    rows = points.shape[0]
    loads = [wires.here(labels, lab.at[0]), wires.here(points, pts.at[pl.ds(0, rows)])]
    old_load = wires.here(old.at[pl.ds(pl.multiple_of(p * 64, 64), 64)], old_rows)

    barrier = pltpu.get_barrier_semaphore()
    for other in partners:
        pl.semaphore_signal(barrier, inc=1, device_id=other, device_id_type=MESH)
    pl.semaphore_wait(barrier, len(partners))
    for load in loads:
        load.wait()

    gathers = []

    def start_gather(t):
        if t < n_chunks:
            block = lambda row, count: pts.at[pl.ds(row, count), pl.ds(STARTS[t], WIDTHS[t])]
            gathers.append(gather_chunk(wires, block, rows, up, down, sibling))
            next(gathers[t])

    label_gather = gather_labels(wires, lab, up, down, across, sibling)
    next(label_gather)
    start_gather(0)
    start_gather(1)

    n_rows = onehot.shape[0]
    first_id = c * n_rows
    tile = 64

    def match(slots):
        @pl.loop(0, n_rows // tile)
        def _(r):
            row = pl.multiple_of(r * tile, tile)
            ids = first_id + row + lax.broadcasted_iota(jnp.int32, (tile, rows), 0)
            for k in slots:
                same = ids == lab[k]
                onehot[pl.ds(row, tile), k * rows : (k + 1) * rows] = jnp.where(same, 1.0, 0.0).astype(BF16)

    def count_digits():
        ones = jnp.ones((onehot.shape[1], DIGITS), BF16)

        @pl.loop(0, 4)
        def _(r):
            row = pl.ds(pl.multiple_of(r * 256, 256), 256)
            count = jnp.dot(onehot[row, :], ones, preferred_element_type=F32).astype(jnp.int32)
            place = lax.broadcasted_iota(jnp.int32, count.shape, 1) & 3
            digit = lax.shift_right_logical(count, place * 4) & 15
            parts[0][r, :, :, SPANS[0][1] :] = digit.astype(F32).astype(BF16).reshape(4, 64, DIGITS)

    def finisher(g, low, size):
        start, width = SPANS[g]
        mine = slice(low, low + size)

        def finish(total):
            if g == 0:
                place = lax.broadcasted_iota(jnp.int32, (size, DIGITS), 1)
                scale = jnp.where(place == 0, 1.0, jnp.where(place == 1, 16.0, jnp.where(place == 2, 256.0, 4096.0)))
                digits = jnp.where(place < 4, total[:, width:] * scale, 0.0)
                count = jnp.sum(digits, axis=1, keepdims=True)
                weights[0, mine] = jnp.broadcast_to(jnp.where(count > 0.0, 0.5 / jnp.maximum(count, 1.0), 0.0), (size, 128))
                weights[1, mine] = jnp.broadcast_to(jnp.where(count > 0.0, 0.5, 1.0), (size, 128))
            old_part = old_rows[mine, start : start + width].astype(F32)
            return (total[:, :width] * weights[0, mine, 0:1] + old_part * weights[1, mine, 0:1]).astype(BF16)

        return finish

    near_rows = 6 * rows
    routes_of, stores = {}, []

    def sum_near(t):
        lanes = slice(STARTS[t], STARTS[t] + WIDTHS[t])

        @pl.loop(0, n_rows // 256)
        def _(r):
            row = pl.ds(pl.multiple_of(r * 256, 256), 256)
            helds[t][row, :] = jnp.dot(onehot[row, 0:near_rows], pts[0:near_rows, lanes], preferred_element_type=F32)

    def sum_far(t):
        lanes = slice(STARTS[t], STARTS[t] + WIDTHS[t])
        g = [t in group for group in GROUPS].index(True)
        to = slice(STARTS[t] - SPANS[g][0], STARTS[t] - SPANS[g][0] + WIDTHS[t])

        @pl.loop(0, 4)
        def _(r):
            row = pl.ds(pl.multiple_of(r * 256, 256), 256)
            sums = jnp.dot(onehot[row, near_rows:], pts[near_rows:, lanes], preferred_element_type=F32)
            parts[g][r, :, :, to] = (helds[t][row, :] + sums).astype(BF16).reshape(4, 64, WIDTHS[t])

    def reduce(g):
        cent = cents.at[:, :, :, pl.ds(*SPANS[g])]
        begin = sum(len(routes) for routes in ROUTES[:g])
        routes_of[g] = [
            reduce_rows(
                wires, axis == "x", low, size, x, z, x_ids, z_ids,
                parts[g], cent, lands[begin + i], lands_two[begin + i], finisher(g, low, size),
            )
            for i, (axis, low, size) in enumerate(ROUTES[g])
        ]
        advance(g)

    def advance(*groups):
        for g in groups:
            for route in routes_of[g]:
                next(route)

    def gathered(t):
        next(gathers[t])

    def store_points(t):
        if STARTS[t] >= EARLY:
            to = pl.ds(STARTS[t] - EARLY, WIDTHS[t])
            stores.append(wires.here(pts.at[:, pl.ds(STARTS[t], WIDTHS[t])], late_points.at[:, to]))

    def store_centroids(g):
        lanes = pl.ds(*SPANS[g])
        stores.append(wires.here(cents.at[:, :, :, lanes], blended.at[:, :, :, lanes]))

    def square_points():
        @pl.loop(0, pts.shape[0] // 256)
        def _(r):
            row = pl.ds(pl.multiple_of(r * 256, 256), 256)
            wide = pts[row, :].astype(F32)
            point_sq[row, :] = jnp.broadcast_to(jnp.sum(wide * wide, axis=1, keepdims=True), (256, point_sq.shape[1]))

    def multiply_early():
        for k, products in enumerate((products_a, products_b, products_c, products_d)):

            @pl.loop(0, 2)
            def _(r):
                row = pl.ds(pl.multiple_of(2 * k * rows + r * rows, rows), rows)
                rhs = cents[:, :, :, 0:EARLY].reshape(n_rows, EARLY)
                products[pl.ds(pl.multiple_of(r * rows, rows), rows), :] = lax.dot_general(
                    pts[row, 0:EARLY], rhs, NT, preferred_element_type=F32
                )

    next(label_gather)
    next(label_gather)
    match(range(4))
    gathered(0)
    start_gather(2)
    match(range(4, 8))
    gathered(0)
    sum_near(0)
    gathered(1)
    start_gather(3)
    count_digits()
    old_load.wait()
    gathered(0)
    gathered(1)
    sum_near(1)
    gathered(0)
    sum_far(0)
    reduce(0)
    gathered(2)
    gathered(1)
    gathered(2)
    sum_near(2)
    gathered(1)
    sum_far(1)
    reduce(1)
    gathered(3)
    advance(0)
    gathered(2)
    gathered(2)
    sum_far(2)
    reduce(2)
    advance(0)
    gathered(3)
    sum_near(3)
    gathered(3)
    advance(1)
    gathered(3)
    sum_far(3)
    reduce(3)
    advance(0)
    store_points(2)
    store_points(3)
    square_points()
    advance(1)
    advance(2)
    advance(3)
    advance(0)
    store_centroids(0)
    advance(1)
    advance(2)
    advance(3)
    wires.settle(20)
    advance(2)
    advance(1)
    store_centroids(1)
    advance(3)
    wires.settle(12)
    multiply_early()
    advance(2)
    store_centroids(2)
    advance(3)
    store_centroids(3)
    wires.settle()
    for copy in stores:
        copy.wait()


def distance_kernel(products_a, products_b, products_c, products_d, points, blended, point_sq, new, out, made, rows_of, staged, sems):
    n_rows, group, block = made.shape[0], points.shape[0], staged.shape[1]
    flat = blended.reshape(n_rows, blended.shape[3])
    tile = 128
    for r in range(n_rows // tile):
        row = pl.ds(r * tile, tile)
        wide = flat[row, :].astype(F32)
        scale = lax.rsqrt(jnp.sum(wide * wide, axis=1, keepdims=True) + 1e-06)
        rounded = (wide * scale).astype(BF16)
        made[row, :] = rounded
        square = jnp.square(rounded.astype(F32))
        cent_sq = jnp.sum(square, axis=1, keepdims=True)
        lane = lax.broadcasted_iota(jnp.int32, (tile, 128), 1)
        rows_of[:, r * tile : (r + 1) * tile] = jnp.where(lane < 8, scale, cent_sq).T
    new_copy = pltpu.make_async_copy(made, new, sems.at[0])
    new_copy.start()
    twice, cent_sq = 2.0 * rows_of[0:1, :], rows_of[8:9, :]

    c = lax.axis_index("cent")
    y, core = c // 2, lax.rem(c, 2)
    copies = []
    for k in range(group // block):
        shift = 2 if k >= 6 else (0, 3, 1)[k % 3]
        side = 1 - core if k in (3, 4, 5, 7) else core
        place = (lax.rem(y + shift, 4) * 2 + side) * block
        slot = k % staged.shape[0]
        if k >= staged.shape[0]:
            for copy in copies[k - staged.shape[0]]:
                copy.wait()
        copies.append([])
        for q in range(2):
            piece = block // 2
            row = slice(k * block + q * piece, k * block + (q + 1) * piece)
            begin = (k % 2) * block + q * piece
            early = (products_a, products_b, products_c, products_d)[k // 2][begin : begin + piece, :]
            late = lax.dot_general(points[row, :], flat[:, EARLY:], NT, preferred_element_type=F32)
            staged[slot, q * piece : (q + 1) * piece] = (point_sq[row, 0:1] + cent_sq) - twice * (early + late)
            to = out.at[pl.ds(pl.multiple_of(place + q * piece, piece), piece)]
            copies[-1].append(pltpu.make_async_copy(staged.at[slot, pl.ds(q * piece, piece)], to, sems.at[1 + 4 * slot + q]))
            copies[-1][-1].start()
    for pieces in copies[-staged.shape[0] :]:
        for copy in pieces:
            copy.wait()
    new_copy.wait()


def shards(points, assign, old_centroids):
    rows, width = points.shape
    n_rows = old_centroids.shape[0]
    labels = assign.reshape(1, rows)
    group = 8 * rows
    n_chunks = len(WIDTHS)
    sums = [w + (DIGITS if g == 0 else 0) for g, (_, w) in enumerate(SPANS)]
    routes = [(size, sums[g]) for g, of_group in enumerate(ROUTES) for _, _, size in of_group]
    n_remote = 6 * n_chunks + 12 * len(routes) + 8
    hbm, vmem = pl.BlockSpec(memory_space=pltpu.HBM), pl.BlockSpec(memory_space=pltpu.VMEM)
    handed_on = pl.pallas_call(
        centroid_kernel,
        out_shape=(
            *[pltpu.VMEM((group // 4, n_rows), F32)] * 4,
            pltpu.VMEM((group, width - EARLY), BF16),
            pltpu.VMEM((4, 4, 64, width), BF16),
            pltpu.VMEM((group, 128), F32),
        ),
        in_specs=[hbm] * 3,
        out_specs=(vmem,) * 7,
        scratch_shapes=[
            pltpu.VMEM((group, width), BF16),
            pltpu.VMEM((8, 1, rows), jnp.int32),
            pltpu.VMEM((n_rows, group), BF16),
            pltpu.VMEM((64, width), BF16),
            pltpu.VMEM((2, 64, 128), F32),
            pltpu.VMEM((4, 4, 64, width), BF16),
            *[pltpu.VMEM((4, 4, 64, w), BF16) for w in sums],
            *[pltpu.VMEM((3, 4, size, w), BF16) for size, w in routes],
            *[pltpu.VMEM((3, size, w), BF16) for size, w in routes],
            *[pltpu.VMEM((n_rows, max(WIDTHS)), F32)] * 2,
            pltpu.SemaphoreType.DMA((n_remote,)),
            pltpu.SemaphoreType.DMA((n_remote,)),
            pltpu.SemaphoreType.DMA((4 + 2 * n_chunks,)),
        ],
        compiler_params=pltpu.CompilerParams(
            collective_id=0, has_side_effects=True, vmem_limit_bytes=26 * 2**20
        ),
        cost_estimate=pl.CostEstimate(flops=3 * n_rows * group * width, bytes_accessed=2 * group * width, transcendentals=0),
    )(*(pltpu.with_memory_space_constraint(a, pltpu.HBM) for a in (points, labels, old_centroids)))
    new_centroids, distances = pl.pallas_call(
        distance_kernel,
        out_shape=(jax.ShapeDtypeStruct((n_rows, width), BF16), jax.ShapeDtypeStruct((group, n_rows), F32)),
        in_specs=[vmem] * 7,
        out_specs=(hbm, hbm),
        scratch_shapes=[
            pltpu.VMEM((n_rows, width), BF16),
            pltpu.VMEM((128, n_rows), F32),
            pltpu.VMEM((3, rows, n_rows), F32),
            pltpu.SemaphoreType.DMA((13,)),
        ],
        compiler_params=pltpu.CompilerParams(vmem_limit_bytes=16 * 2**20),
        cost_estimate=pl.CostEstimate(flops=n_rows * group * width, bytes_accessed=4 * group * n_rows, transcendentals=0),
    )(*(pltpu.with_memory_space_constraint(a, pltpu.VMEM) for a in handed_on))
    return new_centroids, distances


def solution(mesh):
    return jax.shard_map(
        shards,
        mesh=mesh,
        in_specs=(P(("point", "cent"), None), P(("point", "cent")), P("cent", None)),
        out_specs=(P("cent", None), P("point", "cent")),
        check_vma=False,
    )
```

```python
import functools

import jax
import jax.numpy as jnp
from jax import lax
from jax.experimental import pallas as pl
from jax.experimental.pallas import tpu as pltpu
from jax.sharding import PartitionSpec as P

MESH = pl.DeviceIdType.MESH
F32, BF16 = jnp.float32, jnp.bfloat16
NT = (((1,), (1,)), ((), ()))
WIDTHS = (256, 256, 256, 256)
STARTS = tuple(sum(WIDTHS[:t]) for t in range(len(WIDTHS)))
GROUPS = ((0,), (1,), (2,), (3,))
SPANS = tuple((STARTS[g[0]], sum(WIDTHS[t] for t in g)) for g in GROUPS)
ROUTES = ((("x", 0, 32), ("z", 32, 32)),) * 4
EARLY = 512
DIGITS = 128


class Wires:
    def __init__(self, send, recv, local):
        self.send, self.recv, self.local = send, recv, local
        self.n_remote = self.n_local = 0
        self.sent = []

    def remote(self, src, dst, target):
        index = self.n_remote
        self.n_remote += 1
        copy = pltpu.make_async_remote_copy(
            src_ref=src, dst_ref=dst, send_sem=self.send.at[index], recv_sem=self.recv.at[index],
            device_id=target, device_id_type=MESH,
        )
        copy.start()
        self.sent.append(copy)
        return copy

    def settle(self, keep=0):
        count = max(len(self.sent) - keep, 0)
        for copy in self.sent[:count]:
            copy.wait_send()
        del self.sent[:count]

    def here(self, src, dst):
        copy = pltpu.make_async_copy(src, dst, self.local.at[self.n_local])
        self.n_local += 1
        copy.start()
        return copy


def gather_chunk(wires, block, rows, up, down, sibling):
    half = rows // 2
    from_below = wires.remote(block(0, rows), block(rows, rows), up)
    from_above = wires.remote(block(0, rows), block(2 * rows, rows), down)
    yield
    from_below.wait_recv()
    far_a = wires.remote(block(rows, half), block(6 * rows, half), up)
    from_above.wait_recv()
    far_b = wires.remote(block(2 * rows + half, half), block(6 * rows + half, half), down)
    near = wires.remote(block(0, 3 * rows), block(3 * rows, 3 * rows), sibling)
    yield
    near.wait_recv()
    yield
    far_a.wait_recv()
    far_b.wait_recv()
    far = wires.remote(block(6 * rows, rows), block(7 * rows, rows), sibling)
    yield
    far.wait_recv()
    yield


def gather_labels(wires, lab, up, down, across, sibling):
    first = [wires.remote(lab.at[0], lab.at[k], target) for k, target in ((6, across), (1, up), (2, down))]
    near = [wires.remote(lab.at[0], lab.at[3], sibling)]
    yield
    for copy, k, to in zip(first[1:] + first[:1], (1, 2, 6), (4, 5, 7)):
        copy.wait_recv()
        near.append(wires.remote(lab.at[k], lab.at[to], sibling))
    yield
    for copy in near:
        copy.wait_recv()
    yield


def add(*terms):
    total = terms[0].astype(F32)
    for term in terms[1:]:
        total = total + term.astype(F32)
    return total


def reduce_rows(wires, x_first, low, size, x, z, x_ids, z_ids, part, cent, land, land_two, finish):
    order = (2, 1, 3)
    rows = pl.ds(low, size)
    first_ids, second_ids = (x_ids, z_ids) if x_first else (z_ids, x_ids)

    def block(k):
        return (lax.rem(x + k, 4), slice(None), rows) if x_first else (slice(None), lax.rem(z + k, 4), rows)

    def cell(k):
        return (x, lax.rem(z + k, 4), rows) if x_first else (lax.rem(x + k, 4), z, rows)

    copies = [wires.remote(part.at[block(k)], land.at[k - 1], first_ids[k]) for k in order]
    yield
    for copy in copies:
        copy.wait_recv()
    part[block(0)] = add(part[block(0)], land[0], land[1], land[2]).astype(BF16)
    copies = [wires.remote(part.at[cell(k)], land_two.at[k - 1], second_ids[k]) for k in order]
    yield
    for copy in copies:
        copy.wait_recv()
    cent[cell(0)] = finish(add(part[cell(0)], land_two[0], land_two[1], land_two[2]))
    copies = [wires.remote(cent.at[cell(0)], cent.at[cell(0)], second_ids[k]) for k in order]
    yield
    for copy in copies:
        copy.wait_recv()
    copies = [wires.remote(cent.at[block(0)], cent.at[block(0)], first_ids[k]) for k in order]
    yield
    for copy in copies:
        copy.wait_recv()
    yield


def centroid_kernel(points, labels, old, products_a, products_b, products_c, products_d, late_points, blended, point_sq, pts, lab, onehot, old_rows, weights, cents, *rest):
    n_chunks, n_groups = len(WIDTHS), len(GROUPS)
    n_routes = sum(len(routes) for routes in ROUTES)
    parts, rest = rest[:n_groups], rest[n_groups:]
    lands, lands_two, rest = rest[:n_routes], rest[n_routes : 2 * n_routes], rest[2 * n_routes :]
    held_a, held_b, send, recv, local = rest
    helds = [(held_a, held_b)[t % 2].at[:, pl.ds(0, w)] for t, w in enumerate(WIDTHS)]
    wires = Wires(send, recv, local)
    p, c = lax.axis_index("point"), lax.axis_index("cent")
    x, z, y, core = p // 4, lax.rem(p, 4), c // 2, lax.rem(c, 2)

    def ring(k, by):
        return lax.rem(k + 4 + by, 4)

    up, across, down = ({"cent": ring(y, by) * 2 + core} for by in (1, 2, 3))
    sibling = {"cent": y * 2 + 1 - core}
    x_ids = {by: {"point": ring(x, by) * 4 + z} for by in (1, 2, 3)}
    z_ids = {by: {"point": x * 4 + ring(z, by)} for by in (1, 2, 3)}
    partners = (up, across, down, sibling, *x_ids.values(), *z_ids.values())

    rows = points.shape[0]
    loads = [wires.here(labels, lab.at[0]), wires.here(points, pts.at[pl.ds(0, rows)])]
    old_load = wires.here(old.at[pl.ds(pl.multiple_of(p * 64, 64), 64)], old_rows)

    barrier = pltpu.get_barrier_semaphore()
    for other in partners:
        pl.semaphore_signal(barrier, inc=1, device_id=other, device_id_type=MESH)
    pl.semaphore_wait(barrier, len(partners))
    for load in loads:
        load.wait()

    gathers = []

    def start_gather(t):
        if t < n_chunks:
            block = lambda row, count: pts.at[pl.ds(row, count), pl.ds(STARTS[t], WIDTHS[t])]
            gathers.append(gather_chunk(wires, block, rows, up, down, sibling))
            next(gathers[t])

    label_gather = gather_labels(wires, lab, up, down, across, sibling)
    start_gather(0)
    next(label_gather)
    start_gather(1)

    n_rows = onehot.shape[0]
    first_id = c * n_rows
    tile = 64

    def match(slots):
        @pl.loop(0, n_rows // tile)
        def _(r):
            row = pl.multiple_of(r * tile, tile)
            ids = first_id + row + lax.broadcasted_iota(jnp.int32, (tile, rows), 0)
            for k in slots:
                same = ids == lab[k]
                onehot[pl.ds(row, tile), k * rows : (k + 1) * rows] = jnp.where(same, 1.0, 0.0).astype(BF16)

    def count_digits():
        ones = jnp.ones((onehot.shape[1], DIGITS), BF16)

        @pl.loop(0, 4)
        def _(r):
            row = pl.ds(pl.multiple_of(r * 256, 256), 256)
            count = jnp.dot(onehot[row, :], ones, preferred_element_type=F32).astype(jnp.int32)
            place = lax.broadcasted_iota(jnp.int32, count.shape, 1) & 3
            digit = lax.shift_right_logical(count, place * 4) & 15
            parts[0][r, :, :, SPANS[0][1] :] = digit.astype(F32).astype(BF16).reshape(4, 64, DIGITS)

    def finisher(g, low, size):
        start, width = SPANS[g]
        mine = slice(low, low + size)

        def finish(total):
            if g == 0:
                place = lax.broadcasted_iota(jnp.int32, (size, DIGITS), 1)
                scale = jnp.where(place == 0, 1.0, jnp.where(place == 1, 16.0, jnp.where(place == 2, 256.0, 4096.0)))
                digits = jnp.where(place < 4, total[:, width:] * scale, 0.0)
                count = jnp.sum(digits, axis=1, keepdims=True)
                weights[0, mine] = jnp.broadcast_to(jnp.where(count > 0.0, 0.5 / jnp.maximum(count, 1.0), 0.0), (size, 128))
                weights[1, mine] = jnp.broadcast_to(jnp.where(count > 0.0, 0.5, 1.0), (size, 128))
            old_part = old_rows[mine, start : start + width].astype(F32)
            return (total[:, :width] * weights[0, mine, 0:1] + old_part * weights[1, mine, 0:1]).astype(BF16)

        return finish

    near_rows = 6 * rows
    routes_of, stores = {}, []

    def sum_near(t):
        lanes = slice(STARTS[t], STARTS[t] + WIDTHS[t])

        @pl.loop(0, n_rows // 256)
        def _(r):
            row = pl.ds(pl.multiple_of(r * 256, 256), 256)
            helds[t][row, :] = jnp.dot(onehot[row, 0:near_rows], pts[0:near_rows, lanes], preferred_element_type=F32)

    def sum_far(t):
        lanes = slice(STARTS[t], STARTS[t] + WIDTHS[t])
        g = [t in group for group in GROUPS].index(True)
        to = slice(STARTS[t] - SPANS[g][0], STARTS[t] - SPANS[g][0] + WIDTHS[t])

        @pl.loop(0, 4)
        def _(r):
            row = pl.ds(pl.multiple_of(r * 256, 256), 256)
            sums = jnp.dot(onehot[row, near_rows:], pts[near_rows:, lanes], preferred_element_type=F32)
            parts[g][r, :, :, to] = (helds[t][row, :] + sums).astype(BF16).reshape(4, 64, WIDTHS[t])

    def reduce(g):
        cent = cents.at[:, :, :, pl.ds(*SPANS[g])]
        begin = sum(len(routes) for routes in ROUTES[:g])
        routes_of[g] = [
            reduce_rows(
                wires, axis == "x", low, size, x, z, x_ids, z_ids,
                parts[g], cent, lands[begin + i], lands_two[begin + i], finisher(g, low, size),
            )
            for i, (axis, low, size) in enumerate(ROUTES[g])
        ]
        advance(g)

    def advance(*groups):
        for g in groups:
            for route in routes_of[g]:
                next(route)

    def gathered(t):
        next(gathers[t])

    def store_points(t):
        if STARTS[t] >= EARLY:
            to = pl.ds(STARTS[t] - EARLY, WIDTHS[t])
            stores.append(wires.here(pts.at[:, pl.ds(STARTS[t], WIDTHS[t])], late_points.at[:, to]))

    def store_centroids(g):
        lanes = pl.ds(*SPANS[g])
        stores.append(wires.here(cents.at[:, :, :, lanes], blended.at[:, :, :, lanes]))

    def square_points():
        @pl.loop(0, pts.shape[0] // 256)
        def _(r):
            row = pl.ds(pl.multiple_of(r * 256, 256), 256)
            wide = pts[row, :].astype(F32)
            point_sq[row, :] = jnp.broadcast_to(jnp.sum(wide * wide, axis=1, keepdims=True), (256, point_sq.shape[1]))

    def multiply_early():
        for k, products in enumerate((products_a, products_b, products_c, products_d)):

            @pl.loop(0, 2)
            def _(r):
                row = pl.ds(pl.multiple_of(2 * k * rows + r * rows, rows), rows)
                rhs = cents[:, :, :, 0:EARLY].reshape(n_rows, EARLY)
                products[pl.ds(pl.multiple_of(r * rows, rows), rows), :] = lax.dot_general(
                    pts[row, 0:EARLY], rhs, NT, preferred_element_type=F32
                )

    next(label_gather)
    next(label_gather)
    match(range(4))
    gathered(0)
    start_gather(2)
    match(range(4, 8))
    gathered(0)
    sum_near(0)
    gathered(1)
    start_gather(3)
    count_digits()
    old_load.wait()
    gathered(0)
    gathered(1)
    sum_near(1)
    gathered(0)
    sum_far(0)
    reduce(0)
    gathered(2)
    gathered(1)
    gathered(2)
    sum_near(2)
    gathered(1)
    sum_far(1)
    reduce(1)
    gathered(3)
    advance(0)
    gathered(2)
    gathered(2)
    sum_far(2)
    reduce(2)
    advance(0)
    gathered(3)
    sum_near(3)
    gathered(3)
    advance(1)
    gathered(3)
    sum_far(3)
    reduce(3)
    advance(0)
    store_points(2)
    store_points(3)
    square_points()
    advance(1)
    advance(2)
    advance(3)
    advance(0)
    store_centroids(0)
    advance(1)
    advance(2)
    advance(3)
    wires.settle(20)
    advance(2)
    advance(1)
    store_centroids(1)
    advance(3)
    wires.settle(12)
    multiply_early()
    advance(2)
    store_centroids(2)
    advance(3)
    store_centroids(3)
    wires.settle()
    for copy in stores:
        copy.wait()


def distance_kernel(products_a, products_b, products_c, products_d, points, blended, point_sq, new, out, made, rows_of, staged, sems):
    n_rows, group, block = made.shape[0], points.shape[0], staged.shape[1]
    flat = blended.reshape(n_rows, blended.shape[3])
    tile = 128
    for r in range(n_rows // tile):
        row = pl.ds(r * tile, tile)
        wide = flat[row, :].astype(F32)
        scale = lax.rsqrt(jnp.sum(wide * wide, axis=1, keepdims=True) + 1e-06)
        rounded = (wide * scale).astype(BF16)
        made[row, :] = rounded
        square = jnp.square(rounded.astype(F32))
        cent_sq = jnp.sum(square, axis=1, keepdims=True)
        lane = lax.broadcasted_iota(jnp.int32, (tile, 128), 1)
        rows_of[:, r * tile : (r + 1) * tile] = jnp.where(lane < 8, scale, cent_sq).T
    new_copy = pltpu.make_async_copy(made, new, sems.at[0])
    new_copy.start()
    twice, cent_sq = 2.0 * rows_of[0:1, :], rows_of[8:9, :]

    c = lax.axis_index("cent")
    y, core = c // 2, lax.rem(c, 2)
    copies = []
    for k in range(group // block):
        shift = 2 if k >= 6 else (0, 3, 1)[k % 3]
        side = 1 - core if k in (3, 4, 5, 7) else core
        place = (lax.rem(y + shift, 4) * 2 + side) * block
        slot = k % staged.shape[0]
        if k >= staged.shape[0]:
            for copy in copies[k - staged.shape[0]]:
                copy.wait()
        copies.append([])
        for q in range(2):
            piece = block // 2
            row = slice(k * block + q * piece, k * block + (q + 1) * piece)
            begin = (k % 2) * block + q * piece
            early = (products_a, products_b, products_c, products_d)[k // 2][begin : begin + piece, :]
            late = lax.dot_general(points[row, :], flat[:, EARLY:], NT, preferred_element_type=F32)
            staged[slot, q * piece : (q + 1) * piece] = (point_sq[row, 0:1] + cent_sq) - twice * (early + late)
            to = out.at[pl.ds(pl.multiple_of(place + q * piece, piece), piece)]
            copies[-1].append(pltpu.make_async_copy(staged.at[slot, pl.ds(q * piece, piece)], to, sems.at[1 + 4 * slot + q]))
            copies[-1][-1].start()
    for pieces in copies[-staged.shape[0] :]:
        for copy in pieces:
            copy.wait()
    new_copy.wait()


def shards(points, assign, old_centroids):
    rows, width = points.shape
    n_rows = old_centroids.shape[0]
    labels = assign.reshape(1, rows)
    group = 8 * rows
    n_chunks = len(WIDTHS)
    sums = [w + (DIGITS if g == 0 else 0) for g, (_, w) in enumerate(SPANS)]
    routes = [(size, sums[g]) for g, of_group in enumerate(ROUTES) for _, _, size in of_group]
    n_remote = 6 * n_chunks + 12 * len(routes) + 8
    hbm, vmem = pl.BlockSpec(memory_space=pltpu.HBM), pl.BlockSpec(memory_space=pltpu.VMEM)
    handed_on = pl.pallas_call(
        centroid_kernel,
        out_shape=(
            *[pltpu.VMEM((group // 4, n_rows), F32)] * 4,
            pltpu.VMEM((group, width - EARLY), BF16),
            pltpu.VMEM((4, 4, 64, width), BF16),
            pltpu.VMEM((group, 128), F32),
        ),
        in_specs=[hbm] * 3,
        out_specs=(vmem,) * 7,
        scratch_shapes=[
            pltpu.VMEM((group, width), BF16),
            pltpu.VMEM((8, 1, rows), jnp.int32),
            pltpu.VMEM((n_rows, group), BF16),
            pltpu.VMEM((64, width), BF16),
            pltpu.VMEM((2, 64, 128), F32),
            pltpu.VMEM((4, 4, 64, width), BF16),
            *[pltpu.VMEM((4, 4, 64, w), BF16) for w in sums],
            *[pltpu.VMEM((3, 4, size, w), BF16) for size, w in routes],
            *[pltpu.VMEM((3, size, w), BF16) for size, w in routes],
            *[pltpu.VMEM((n_rows, max(WIDTHS)), F32)] * 2,
            pltpu.SemaphoreType.DMA((n_remote,)),
            pltpu.SemaphoreType.DMA((n_remote,)),
            pltpu.SemaphoreType.DMA((4 + 2 * n_chunks,)),
        ],
        compiler_params=pltpu.CompilerParams(
            collective_id=0, has_side_effects=True, vmem_limit_bytes=26 * 2**20
        ),
        cost_estimate=pl.CostEstimate(flops=3 * n_rows * group * width, bytes_accessed=2 * group * width, transcendentals=0),
    )(*(pltpu.with_memory_space_constraint(a, pltpu.HBM) for a in (points, labels, old_centroids)))
    new_centroids, distances = pl.pallas_call(
        distance_kernel,
        out_shape=(jax.ShapeDtypeStruct((n_rows, width), BF16), jax.ShapeDtypeStruct((group, n_rows), F32)),
        in_specs=[vmem] * 7,
        out_specs=(hbm, hbm),
        scratch_shapes=[
            pltpu.VMEM((n_rows, width), BF16),
            pltpu.VMEM((128, n_rows), F32),
            pltpu.VMEM((3, rows, n_rows), F32),
            pltpu.SemaphoreType.DMA((13,)),
        ],
        compiler_params=pltpu.CompilerParams(vmem_limit_bytes=16 * 2**20),
        cost_estimate=pl.CostEstimate(flops=n_rows * group * width, bytes_accessed=4 * group * n_rows, transcendentals=0),
    )(*(pltpu.with_memory_space_constraint(a, pltpu.VMEM) for a in handed_on))
    return new_centroids, distances


def solution(mesh):
    return jax.shard_map(
        shards,
        mesh=mesh,
        in_specs=(P(("point", "cent"), None), P(("point", "cent")), P("cent", None)),
        out_specs=(P("cent", None), P("point", "cent")),
        check_vma=False,
    )
```
